32 devices in a mesh: row: 4 (over y, core), col: 8 (over z, x).
Axes of the slice: x: 2, y: 2, z: 4, core: 2. Of those that a mesh axis runs over, the one named last changes fastest.
Arguments:
- transition: bfloat16 [32768, 32768], P('row', 'col'), may hold values from 1.5258789e-06 to 0.0024414062, as said below
- emission: bfloat16 [96, 32768], P(None, 'col'), may hold values from 0.0099487305 to 1
- token_ids: int32 [2, 192], replicated, may hold values from 0 to 95
- forward: bfloat16 [2, 192, 32768], P(None, 'col', 'row'), may hold values from 3.0517578e-06 to 0.0008239746, as said below
- backward_last: float32 [192, 32768], P('row', 'col'), may hold values from 0.1 to 10
Outputs:
- backward: float32 [2, 192, 32768], P(None, 'col', 'row')
- counts: float32 [32768, 1024], P('row', 'col')
The draws below stay inside these ranges and needn't reach their ends.
Inputs may be any that keep to these rules, and one draw needn't show every extreme that they name: Positive transition weights. Positive forward weights.
All inputs are finite; a program needn't handle non-finite values.
Results may differ from the reference program's by a relative error of at most 0.00048.
Values may be sent and summed in bfloat16 or wider, within the bound.
A program may use at most 192 MiB of HBM per device.

```python
import math
import jax
import jax.numpy as jnp
from jax import lax

H = 32768
N = 192
DW = 128
U = 96
N_COL = 8


def draw_transition(key, part):
    base_key, pair_key, factor_key = jax.random.split(key, 3)
    pairing = jax.random.permutation(pair_key, 32)
    source_block = jnp.arange(H) * 16 // H
    dest_block = pairing[jnp.arange(H) * 32 // H] % 16
    boost = jnp.where(source_block[:, None] == dest_block[None, :], 4.0, 1.0)
    row_factor = jnp.exp(jax.random.uniform(factor_key, (H,), jnp.float32, math.log(0.125), math.log(8.0)))
    base = jnp.exp(jax.random.uniform(base_key, (H, H), jnp.float32, math.log(0.4), math.log(2.5)))
    return (base * row_factor[:, None] * boost / H).astype(jnp.bfloat16)


def draw_forward(key, part):
    states = jnp.arange(H).astype(jnp.float32) / H
    base = jnp.exp(jax.random.uniform(key, (2, N, H), jnp.float32, math.log(0.3), math.log(3.0)))
    ramp = 1.0 + 2.0 * states
    return (base * ramp[None, None, :] / H).astype(jnp.bfloat16)


def touch_ends(entries, own_key, smallest, top_value):
    longest = entries.shape.index(max(entries.shape))
    spots = []
    for shift in (0, 1):
        where = [jax.random.randint(jax.random.fold_in(own_key, axis), (), 0, length) for axis, length in enumerate(entries.shape)]
        where[longest] = (where[longest] + shift) % entries.shape[longest]
        spots.append(tuple(where))
    return entries.at[spots[0]].set(smallest).at[spots[1]].set(top_value)


def level_of(own_key, shape, cuts, low, largest):
    def one(axis_at, parts):
        heights = jax.random.uniform(jax.random.fold_in(jax.random.fold_in(own_key, 6), axis_at), (parts,), jnp.float32, low / len(cuts), largest / len(cuts))
        return jnp.repeat(jnp.exp(heights), shape[axis_at] // parts).reshape((-1,) + (1,) * (len(shape) - axis_at - 1))

    factor_of = one(*cuts[0])
    for cut in cuts[1:]:
        factor_of = factor_of * one(*cut)
    return factor_of


def setup_inputs(seed: int = 0) -> dict:
    key_list = jax.random.split(jax.random.key(seed), 6)
    transition = draw_transition(jax.random.fold_in(key_list[5], 71), 0)
    emission = jnp.clip(jnp.exp(math.log(1.0) - 4.61031033 * jax.random.uniform(key_list[1], (U, H), jnp.float32) ** level_of(key_list[1], (U, H), ((1, 8),), -0.2, 0.2)), 0.0099487305, 1.0).astype(jnp.bfloat16)
    token_ids = touch_ends(jax.random.randint(key_list[2], (2, N), 0, U), jax.random.fold_in(key_list[2], 1), 0, U - 1).astype(jnp.int32)
    forward = draw_forward(jax.random.fold_in(key_list[5], 71), 0)
    backward_last = jnp.clip(jnp.exp(math.log(10.0) - 4.6051702 * jax.random.uniform(key_list[4], (N, H), jnp.float32) ** level_of(key_list[4], (N, H), ((0, 4), (1, 8)), -0.2, 0.2)), 0.1, 10.0)
    return {"transition": transition, "emission": emission, "token_ids": token_ids, "forward": forward, "backward_last": backward_last}


def reference(transition, emission, token_ids, forward, backward_last):
    block_dst = H // N_COL
    window = transition.reshape(H, N_COL, block_dst)[:, :, :DW].reshape(H, N_COL * DW)
    totals = jnp.zeros((H, N_COL * DW), jnp.float32)
    backward_next = backward_last
    results = [None, None]
    for step in (1, 0):
        emitted = jnp.take(emission, token_ids[step], axis=0).astype(jnp.float32)
        weighted_back = (emitted * backward_next).astype(jnp.bfloat16)
        summed = lax.dot_general(weighted_back, transition, (((1,), (1,)), ((), ())), preferred_element_type=jnp.float32)
        alpha = forward[step].astype(jnp.float32)
        normal = jnp.sum(alpha * summed, axis=1)
        results[step] = summed / normal[:, None]
        scaled = (alpha / normal[:, None]).astype(jnp.bfloat16)
        picked = weighted_back.reshape(N, N_COL, block_dst)[:, :, :DW].reshape(N, N_COL * DW)
        totals = totals + jnp.dot(scaled.T, picked, preferred_element_type=jnp.float32)
        backward_next = results[step]
    counts = window.astype(jnp.float32) * totals * (H * H / N)
    return jnp.stack(results), counts
```

```python
import functools
import math

import jax
import jax.numpy as jnp
from jax import lax
from jax.experimental import pallas as pl
from jax.experimental.pallas import tpu as pltpu
from jax.sharding import PartitionSpec as P

H = 32768
N = 192
DW = 128
CHUNKS = 2
A_MIN, A_MAX = 1.5258789e-06, 0.0024414062
E_MIN, E_MAX = 0.0099487305, 1.0
B_MIN, B_MAX = 0.1, 10.0
F_MIN, F_MAX = 3.0517578e-06, 0.0008239746
CHUNK = 1024
SLOTS = 4
MESH = pl.DeviceIdType.MESH


def code_range(lo, hi):
    low = math.log2(lo) - 0.5
    high = math.log2(hi) + 0.5
    return 65000.0 / (high - low), (high + low) / 2


def encode(value, slope, middle):
    return jnp.round(jnp.log2(value) * slope - slope * middle).astype(jnp.int32).astype(jnp.int16)


def decode(code, slope, middle):
    return jnp.exp2(code.astype(jnp.int32).astype(jnp.float32) * (1.0 / slope) + middle)


def step_kernel(slope, middle, g_ref, a_ref, u_ref, a_buf, p_buf, q_buf, r_buf, xs, xr, ys, yr, zs, zr, a_sem, x_sem, y_sem, z_sem):
    count = xs.shape[0]
    slots, chunk = a_buf.shape[0], a_buf.shape[1]
    seqs = p_buf.shape[4]
    half = chunk // 2
    me = lax.axis_index("col")
    bx, by, bz = me % 2, (me // 2) % 2, me // 4
    px = me + 1 - 2 * bx
    py = me + 2 - 4 * by
    pz = me + 4 - 8 * bz
    enc = functools.partial(encode, slope=slope, middle=middle)
    dec = functools.partial(decode, slope=slope, middle=middle)

    def load(m):
        slot = lax.rem(m, slots)
        rows = pl.ds(pl.multiple_of(m * chunk, chunk), chunk)
        return pltpu.make_async_copy(a_ref.at[rows], a_buf.at[slot], a_sem.at[slot])

    def move(src, dst, sem, m, to):
        return pltpu.make_async_remote_copy(
            src_ref=src.at[m], dst_ref=dst.at[m], send_sem=sem.at[0, m], recv_sem=sem.at[1, m],
            device_id={"col": to}, device_id_type=MESH,
        )

    for m in range(min(slots, count)):
        load(m).start()
    barrier = pltpu.get_barrier_semaphore()
    for to in (px, py, pz):
        pl.semaphore_signal(barrier, inc=1, device_id={"col": to}, device_id_type=MESH)
    pl.semaphore_wait(barrier, 3)

    def body(m, carry):
        @pl.when(m < count)
        def _():
            load(m).wait()
            slot = lax.rem(m, 2)
            part = lax.dot_general(
                g_ref[...], a_buf[lax.rem(m, slots)], (((1,), (1,)), ((), ())), preferred_element_type=jnp.float32
            )
            p_buf[slot] = part.reshape(p_buf.shape[1:])

            @pl.when(m + slots < count)
            def _():
                load(m + slots).start()

            away = p_buf[slot, :, :, 1 - bx].reshape(4 * seqs, chunk)
            xs[m] = enc(away)
            move(xs, xr, x_sem, m, px).start()

        @pl.when((m >= 1) & (m < count + 1))
        def _():
            n = m - 1
            move(xs, xr, x_sem, n, px).wait()
            got = dec(xr[n]).reshape(2, 2, seqs, chunk)
            q_buf[...] = p_buf[lax.rem(n, 2), :, :, bx] + got
            ys[n] = enc(q_buf[:, 1 - by].reshape(2 * seqs, chunk))
            move(ys, yr, y_sem, n, py).start()
            r_buf[lax.rem(n, 2)] = q_buf[:, by]

        @pl.when((m >= 2) & (m < count + 2))
        def _():
            n = m - 2
            move(ys, yr, y_sem, n, py).wait()
            got = dec(yr[n]).reshape(2, seqs, chunk)
            r_buf[lax.rem(n, 2)] += got
            away = r_buf[lax.rem(n, 2), 1 - bz]
            zs[n] = enc(jnp.concatenate([away[:, :half], away[:, half:]], axis=0))
            move(zs, zr, z_sem, n, pz).start()
            cols = pl.ds(pl.multiple_of(n * chunk, chunk), chunk)
            u_ref[:, cols] = r_buf[lax.rem(n, 2), bz]

        @pl.when(m >= 3)
        def _():
            n = m - 3
            move(zs, zr, z_sem, n, pz).wait()
            got = dec(zr[n])
            cols = pl.ds(pl.multiple_of(n * chunk, chunk), chunk)
            u_ref[:, cols] += jnp.concatenate([got[:seqs], got[seqs:]], axis=1)

        return carry

    lax.fori_loop(0, count + 3, body, 0)


def step_product(g, transition, lo, hi, seqs, ident):
    rows, depth = transition.shape
    chunk = CHUNK
    count = rows // chunk
    slope, middle = code_range(lo, hi)
    i16 = jnp.int16
    return pl.pallas_call(
        functools.partial(step_kernel, slope, middle),
        out_shape=jax.ShapeDtypeStruct((seqs, rows), jnp.float32),
        in_specs=[pl.BlockSpec(memory_space=pltpu.VMEM), pl.BlockSpec(memory_space=pl.ANY)],
        out_specs=pl.BlockSpec(memory_space=pltpu.VMEM),
        scratch_shapes=[
            pltpu.VMEM((SLOTS, chunk, depth), jnp.bfloat16),
            pltpu.VMEM((2, 2, 2, 2, seqs, chunk), jnp.float32),
            pltpu.VMEM((2, 2, seqs, chunk), jnp.float32),
            pltpu.VMEM((2, 2, seqs, chunk), jnp.float32),
            pltpu.VMEM((count, 4 * seqs, chunk), i16),
            pltpu.VMEM((count, 4 * seqs, chunk), i16),
            pltpu.VMEM((count, 2 * seqs, chunk), i16),
            pltpu.VMEM((count, 2 * seqs, chunk), i16),
            pltpu.VMEM((count, 2 * seqs, chunk // 2), i16),
            pltpu.VMEM((count, 2 * seqs, chunk // 2), i16),
            pltpu.SemaphoreType.DMA((SLOTS,)),
            pltpu.SemaphoreType.DMA((2, count)),
            pltpu.SemaphoreType.DMA((2, count)),
            pltpu.SemaphoreType.DMA((2, count)),
        ],
        cost_estimate=pl.CostEstimate(flops=2 * 8 * seqs * rows * depth, bytes_accessed=2 * rows * depth, transcendentals=0),
        compiler_params=pltpu.CompilerParams(collective_id=ident, has_side_effects=True, vmem_limit_bytes=56 << 20),
    )(g, transition)


def in_order(arrived, index):
    count = len(arrived)
    turned = jnp.stack([arrived[-i % count] for i in range(count)] * 2)
    return lax.dynamic_slice_in_dim(turned, (count - index) % count, count, 0)


def gather_small(value, col_count, col_index):
    arrived = [value]
    for k in range(1, col_count):
        arrived.append(lax.ppermute(value, "col", [(c, (c + k) % col_count) for c in range(col_count)]))
    place = lax.broadcasted_iota(jnp.int32, (col_count,) + value.shape, 0)
    out = jnp.zeros(place.shape, value.dtype)
    for k, got in enumerate(arrived):
        out = jnp.where(place == (col_index - k + col_count) % col_count, got[None], out)
    return out


def gather_rows(value, row_count, row_index):
    half = row_count // 2
    arrived = [value]
    for k in range(1, half):
        arrived.append(lax.ppermute(value, "row", [(r, (r + 2 * k) % row_count) for r in range(row_count)]))
    own = in_order(arrived, row_index // 2) if half > 1 else value[None]
    got = lax.ppermute(own, "row", [(r, r ^ 1) for r in range(row_count)])
    even = row_index % 2 == 0
    both = jnp.stack([jnp.where(even, own, got), jnp.where(even, got, own)], axis=1)
    return both.reshape(row_count * value.shape[0], value.shape[1])


def split_pair(partial, scale, col_count, col_index, local_seqs):
    scaled = (partial * scale).reshape(col_count // 2, 2, local_seqs, partial.shape[1])
    side = col_index % 2
    away = lax.dynamic_index_in_dim(scaled, 1 - side, 1, keepdims=False).astype(jnp.float16)
    return away, lax.dynamic_index_in_dim(scaled, side, 1, keepdims=False)


def reduce_scatter(away, keep, col_count, col_index):
    half = col_count // 2
    got = lax.ppermute(away, "col", [(c, c ^ 1) for c in range(col_count)])
    pair = keep + got.astype(jnp.float32)
    here = col_index // 2
    total = lax.dynamic_index_in_dim(pair, here, 0, keepdims=False)
    packed = pair.astype(jnp.float16)
    for k in range(1, half):
        piece = lax.dynamic_index_in_dim(packed, (here + k) % half, 0, keepdims=False)
        got = lax.ppermute(piece, "col", [(c, (c + 2 * k) % col_count) for c in range(col_count)])
        total = total + got.astype(jnp.float32)
    return total


def plain_product(weighted_back, transition, scale, scale_mine, col_count, col_index, local_seqs):
    chunk = transition.shape[0] // CHUNKS
    pieces = []
    for k in range(CHUNKS):
        rows = slice(k * chunk, (k + 1) * chunk)
        partial = lax.dot_general(
            weighted_back, transition[rows], (((1,), (1,)), ((), ())), preferred_element_type=jnp.float32
        )
        away, keep = split_pair(partial, scale, col_count, col_index, local_seqs)
        if k < CHUNKS - 1:
            weighted_back, away = lax.optimization_barrier((weighted_back, away))
        pieces.append(reduce_scatter(away, keep, col_count, col_index))
    return jnp.concatenate(pieces, axis=1) / scale_mine


def on_device(transition, emission, token_ids, forward, backward_last):
    row_count = lax.axis_size("row")
    col_count = lax.axis_size("col")
    row_index = lax.axis_index("row")
    col_index = lax.axis_index("col")
    ratio = col_count // row_count
    local_seqs = forward.shape[1]
    row_seqs = backward_last.shape[0]
    block_src = transition.shape[0]
    block_dst = transition.shape[1]
    seq_total = local_seqs * col_count
    columns = lax.broadcasted_iota(jnp.int32, (row_seqs, emission.shape[0]), 1)
    window = transition[:, :DW]
    outputs = [None, None]
    normals = [None, None]
    picked = [None, None]
    beta = backward_last
    scale = jnp.full((seq_total, 1), 64.0, jnp.float32)
    scale_mine = jnp.full((local_seqs, 1), 64.0, jnp.float32)
    for step in (1, 0):
        tokens = lax.dynamic_slice_in_dim(token_ids[step], row_index * row_seqs, row_seqs, 0)
        onehot = (tokens[:, None] == columns).astype(jnp.bfloat16)
        emitted = jnp.dot(onehot, emission, preferred_element_type=jnp.float32)
        local_back = (emitted * beta).astype(jnp.bfloat16)
        weighted_back = gather_rows(local_back, row_count, row_index)
        picked[step] = weighted_back[:, :DW]
        if step == 1:
            forward_all = lax.all_gather(forward, "col", axis=1, tiled=True)
        if step == 1:
            lo = block_dst * A_MIN * E_MIN * B_MIN
            hi = H * A_MAX * E_MAX * B_MAX
        else:
            lo = block_dst * A_MIN * E_MIN * (A_MIN / A_MAX) / (H * F_MAX)
            hi = H * A_MAX * E_MAX * (A_MAX / A_MIN) / (H * F_MIN)
        if col_count == 8 and local_seqs % 8 == 0:
            mine = step_product(weighted_back, transition, lo, hi, local_seqs, step)
        else:
            mine = plain_product(weighted_back, transition, scale, scale_mine, col_count, col_index, local_seqs)
        norm = jnp.sum(forward[step].astype(jnp.float32) * mine, axis=1)
        sums = lax.psum(jnp.stack([norm, jnp.sum(mine, axis=1)]), "row")
        sums_all = gather_small(sums, col_count, col_index)
        normals[step] = sums_all[:, 0].reshape(seq_total)
        outputs[step] = mine / sums[0][:, None]
        if step == 1:
            halves = outputs[step].reshape(local_seqs, ratio, block_dst)
            arrived = []
            for p in range(ratio):
                part = lax.dynamic_index_in_dim(halves, (col_index + p) % ratio, 1, keepdims=False)
                moves = []
                for r in range(row_count):
                    for c in range(col_count):
                        moves.append((r * col_count + c, (c // ratio) * col_count + r * ratio + (c + p) % ratio))
                arrived.append(lax.ppermute(part, ("row", "col"), moves))
            beta = in_order(arrived, col_index % ratio).reshape(row_seqs, block_dst)
            scale = (16777216.0 * sums_all[:, 0] / sums_all[:, 1]).reshape(seq_total, 1)
            scale_mine = (16777216.0 * sums[0] / sums[1])[:, None]
    totals = jnp.zeros((block_src, DW), jnp.float32)
    for step in (1, 0):
        scaled = (forward_all[step].astype(jnp.float32) / normals[step][:, None]).astype(jnp.bfloat16)
        totals = totals + lax.dot_general(
            scaled, picked[step], (((0,), (0,)), ((), ())), preferred_element_type=jnp.float32
        )
    counts = window.astype(jnp.float32) * totals * (H * H / N)
    return (jnp.stack(outputs), counts)


def solution(mesh):
    in_specs = (P("row", "col"), P(None, "col"), P(), P(None, "col", "row"), P("row", "col"))
    out_specs = (P(None, "col", "row"), P("row", "col"))
    return jax.shard_map(
        on_device, mesh=mesh, in_specs=in_specs, out_specs=out_specs, check_vma=False
    )
```

```python
import functools
import math

import jax
import jax.numpy as jnp
from jax import lax
from jax.experimental import pallas as pl
from jax.experimental.pallas import tpu as pltpu
from jax.sharding import PartitionSpec as P

H = 32768
N = 192
DW = 128
CHUNKS = 2
A_MIN, A_MAX = 1.5258789e-06, 0.0024414062
E_MIN, E_MAX = 0.0099487305, 1.0
B_MIN, B_MAX = 0.1, 10.0
CHUNK = 512
SLOTS = 4
MESH = pl.DeviceIdType.MESH


def code_range(lo, hi):
    low = math.log2(lo) - 0.5
    high = math.log2(hi) + 0.5
    return 65000.0 / (high - low), (high + low) / 2


def encode(value, slope, middle):
    return jnp.round(jnp.log2(value) * slope - slope * middle).astype(jnp.int32).astype(jnp.int16)


def decode(code, slope, middle):
    return jnp.exp2(code.astype(jnp.int32).astype(jnp.float32) * (1.0 / slope) + middle)


def big_kernel(
    codes, hot1_ref, hot0_ref, emit_ref, last_ref, fwd_ref, a_ref,
    u_ref, zall_ref, gw_ref, fall_ref,
    a_buf, p_buf, q_buf, g1, g0, zacc, zs, zr, zc, us, ug,
    xs, xr, as_, ar, bs, br, cs, cr,
    a_sem, x_sem, al_sem, b_sem, c_sem, gy_sem, gc_sem, gd_sem, us_sem, ug_sem, uc_sem, zr_sem, zc_sem, fx_sem, fz_sem,
):
    count = xs.shape[1]
    slots, chunk = a_buf.shape[0], a_buf.shape[1]
    seqs = q_buf.shape[2]
    half = chunk // 2
    per = count // 2
    deep = q_buf.shape[0]
    r = lax.axis_index("row")
    c = lax.axis_index("col")
    y, k, z, x = r // 2, r % 2, c // 2, c % 2
    side = z // 2
    outer = (z == 0) | (z == 3)
    z_in, z_out = 1 + side, 3 * side
    z_in2, z_out2 = 2 - side, 3 - 3 * side
    px = 2 * z + 1 - x
    r1, r2 = r + 1 - 2 * k, (r + 2) % 4
    part_cols = g1.shape[2] // 4

    def remote(src, dst, send, recv, row, col):
        return pltpu.make_async_remote_copy(
            src_ref=src, dst_ref=dst, send_sem=send, recv_sem=recv,
            device_id={"row": row, "col": col}, device_id_type=MESH,
        )

    def load(g):
        slot = lax.rem(g, slots)
        n = lax.rem(g, count)
        at = pl.ds(pl.multiple_of(((n % 2) * per + n // 2) * chunk, chunk), chunk)
        return pltpu.make_async_copy(a_ref.at[at], a_buf.at[slot], a_sem.at[slot])

    for g in range(slots):
        load(g).start()
    barrier = pltpu.get_barrier_semaphore()
    me = r * 8 + c

    def greet(i, carry):
        @pl.when(i != me)
        def _():
            pl.semaphore_signal(barrier, inc=1, device_id={"row": i // 8, "col": i % 8}, device_id_type=MESH)
        return carry

    lax.fori_loop(0, 32, greet, 0)

    for j in range(4):
        cols = slice(j * part_cols, (j + 1) * part_cols)
        emitted = jnp.dot(hot1_ref[...], emit_ref[:, cols], preferred_element_type=jnp.float32)
        g1[r, :, cols] = (emitted * last_ref[:, cols]).astype(jnp.bfloat16)
    wide = fall_ref.shape[3]
    for time in range(2):
        for j in range(4):
            left = slice(j * wide // 4, (j + 1) * wide // 4)
            right = slice(wide + j * wide // 4, wide + (j + 1) * wide // 4)
            pair = [fwd_ref[time, :, left].astype(jnp.float32), fwd_ref[time, :, right].astype(jnp.float32)]
            fall_ref[time, c, :, left] = jnp.concatenate(pair, axis=0).astype(jnp.bfloat16)
    pl.semaphore_wait(barrier, 31)

    def g_move(block, j, sem, to):
        at = g1.at[block, :, pl.ds(j * part_cols, part_cols)]
        return remote(at, at, sem.at[0, j], sem.at[1, j], to, c)

    for j in range(4):
        g_move(r, j, gy_sem, r2).start()
        g_move(r, j, gc_sem, r1).start()

    def fx_move(i, t, block):
        at = fall_ref.at[t, block]
        return remote(at, at, fx_sem.at[0, i], fx_sem.at[1, i], r, px)

    def fz_move(way, kind, src, to):
        t = 0 if kind == 0 else 1
        block = 2 * src + (x if kind < 2 else 1 - x)
        at = fall_ref.at[t, block]
        return remote(at, at, fz_sem.at[0, way, kind, src], fz_sem.at[1, way, kind, src], r, 2 * to + x)

    def fz_send(kind, d):
        @pl.when((z < 3) & (z - d + 1 >= 0))
        def _():
            fz_move(0, kind, z - d + 1, z + 1).start()

        @pl.when((z > 0) & (z + d - 1 <= 3))
        def _():
            fz_move(1, kind, z + d - 1, z - 1).start()

    def fz_sent(kind, d):
        @pl.when((z < 3) & (z - d + 1 >= 0))
        def _():
            fz_move(0, kind, z - d + 1, z + 1).wait_send()

        @pl.when((z > 0) & (z + d - 1 <= 3))
        def _():
            fz_move(1, kind, z + d - 1, z - 1).wait_send()

    def fz_got(kind, d):
        @pl.when(z - d >= 0)
        def _():
            fz_move(0, kind, z - d, z).wait_recv()

        @pl.when(z + d <= 3)
        def _():
            fz_move(1, kind, z + d, z).wait_recv()

    def fx_each(d, act):
        @pl.when(z - d >= 0)
        def _():
            act(fx_move(1 + z - d, 0, 2 * (z - d) + x))

        if d:
            @pl.when(z + d <= 3)
            def _():
                act(fx_move(1 + z + d, 0, 2 * (z + d) + x))

    def start(move):
        move.start()

    fx_move(0, 1, c).start()
    fz_send(0, 1)
    for j in range(4):
        g_move(r, j, gy_sem, r2).wait_recv()
        g_move(r2, j, gd_sem, r1).start()
    for j in range(4):
        g_move(r, j, gc_sem, r1).wait()
        g_move(r2, j, gd_sem, r1).wait()
        g_move(r, j, gy_sem, r2).wait_send()
    fx_each(0, start)
    fx_move(0, 1, c).wait_recv()
    fz_send(1, 1)
    fz_send(2, 1)

    def tick1a():
        fz_got(0, 1)
        fz_send(0, 2)

    def tick1b():
        for kind in (1, 2):
            fz_got(kind, 1)
            fz_send(kind, 2)

    def tick1c():
        fz_got(0, 2)
        fz_send(0, 3)
        fx_each(1, start)

    def tick1d():
        fx_each(2, start)

    def tick0a():
        for kind in (1, 2):
            fz_got(kind, 2)
            fz_send(kind, 3)

    def tick0b():
        fz_got(0, 3)
        fx_each(3, start)

    def two(value):
        return jnp.concatenate([value[:, :half], value[:, half:]], axis=0)

    def one(value):
        n = value.shape[0] // 2
        return jnp.concatenate([value[:n], value[n:]], axis=1)

    zacc[...] = jnp.zeros(zacc.shape, jnp.float32)

    def run(ti, g_buf, ticks):
        time = 1 - ti
        slope, middle = codes[ti]
        enc = functools.partial(encode, slope=slope, middle=middle)
        dec = functools.partial(decode, slope=slope, middle=middle)

        def x_move(n):
            return remote(xs.at[ti, n], xr.at[ti, n], x_sem.at[0, ti, n], x_sem.at[1, ti, n], r, px)

        def a_move(n):
            return remote(as_.at[ti, n], ar.at[ti, n], al_sem.at[0, ti, n], al_sem.at[1, ti, n], r, 2 * z_in + x)

        def b_move(n):
            return remote(bs.at[ti, n], br.at[ti, n], b_sem.at[0, ti, n], b_sem.at[1, ti, n], r, 2 * z_in2 + x)

        def c_move(n):
            return remote(cs.at[ti, n], cr.at[ti, n], c_sem.at[0, ti, n], c_sem.at[1, ti, n], r, 2 * z_out + x)

        def u_move(n, yy, to_col, q):
            return remote(us.at[n], ug.at[q, c], us_sem.at[yy, n], ug_sem.at[q, c], 2 * yy + k, to_col)

        def uc_move(q):
            return remote(ug.at[q], ug.at[q], uc_sem.at[0, q], uc_sem.at[1, q], r1, c)

        def body(m, carry):
            @pl.when(m < count)
            def _():
                g = m + ti * count
                load(g).wait()
                part = lax.dot_general(
                    g_buf[...].reshape(8 * seqs, g_buf.shape[-1]), a_buf[lax.rem(g, slots)], (((1,), (1,)), ((), ())),
                    preferred_element_type=jnp.float32,
                )
                p_buf[...] = part.reshape(p_buf.shape)

                @pl.when(g + slots < 2 * count)
                def _():
                    load(g + slots).start()

                xs[ti, m] = enc(p_buf[:, 1 - x].reshape(4 * seqs, chunk))
                x_move(m).start()
                q_buf[lax.rem(m, deep)] = p_buf[:, x]

            for at, act in ticks:
                pl.when(m == at)(act)

            @pl.when((m >= LAG) & (m < count + LAG))
            def _():
                n = m - LAG
                s = lax.rem(n, deep)
                x_move(n).wait()
                q_buf[s] += dec(xr[ti, n]).reshape(4, seqs, chunk)

                @pl.when(outer)
                def _():
                    three = jnp.concatenate([q_buf[s, z_in], q_buf[s, z_in2], q_buf[s, z_out2]], axis=0)
                    as_[ti, n] = enc(two(three))
                    a_move(n).start()

            @pl.when((m >= 2 * LAG) & (m < count + 2 * LAG) & jnp.logical_not(outer))
            def _():
                n = m - 2 * LAG
                s = lax.rem(n, deep)
                a_move(n).wait_recv()
                got = one(dec(ar[ti, n]))
                q_buf[s, z_in] += got[:seqs]
                pair = jnp.concatenate([q_buf[s, z_in2] + got[seqs:2 * seqs], q_buf[s, z_out2] + got[2 * seqs:]], axis=0)
                bs[ti, n] = enc(pair)
                b_move(n).start()

            @pl.when((m >= 3 * LAG) & (m < count + 3 * LAG) & jnp.logical_not(outer))
            def _():
                n = m - 3 * LAG
                s = lax.rem(n, deep)
                b_move(n).wait()
                got = dec(br[ti, n])
                q_buf[s, z_in] += got[:seqs]
                cs[ti, n] = enc(two(q_buf[s, z_out] + got[seqs:]))
                c_move(n).start()

            @pl.when((m >= 4 * LAG) & (m < count + 4 * LAG))
            def _():
                n = m - 4 * LAG
                s = lax.rem(n, deep)

                @pl.when(outer)
                def _():
                    c_move(n).wait_recv()
                    a_move(n).wait_send()
                    q_buf[s, z_out] += one(dec(cr[ti, n]))

                @pl.when(jnp.logical_not(outer))
                def _():
                    c_move(n).wait_send()

                value = q_buf[s, z]
                cols = pl.ds(pl.multiple_of(((n % 2) * per + n // 2) * chunk, chunk), chunk)
                u_ref[time, :, cols] = value
                weighed = fwd_ref[time, :, cols].astype(jnp.float32) * value
                total = zacc[time]
                for i in range(chunk // 128):
                    total = total + weighed[:, i * 128:(i + 1) * 128]
                zacc[time] = total
                if ti == 0:
                    h = n % 2
                    q = n // 2
                    to_col = 2 * r + h
                    us[n] = enc(two(value))
                    for yy in range(2):
                        mine = (yy == y) & (to_col == c)

                        @pl.when(mine)
                        def _():
                            ug[q, c] = us[n]

                        @pl.when(jnp.logical_not(mine))
                        def _():
                            u_move(n, yy, to_col, q).start()

            if ti == 0:
                ahead = m - (4 * LAG + GAP + x)
                direct = k == z % 2

                @pl.when((ahead >= 0) & (ahead < 2 * per) & (ahead % 2 == 0) & direct)
                def _():
                    q = ahead // 2
                    for src in range(8):
                        @pl.when(jnp.logical_not((r == z) & (c == src)))
                        def _():
                            remote(us.at[0], ug.at[q, src], us_sem.at[0, 0], ug_sem.at[q, src], r, src).wait_recv()
                    uc_move(q).start()

                later = ahead - GAP2

                @pl.when((later >= 0) & (later < 2 * per) & (later % 2 == 0))
                def _():
                    q = later // 2

                    @pl.when(direct)
                    def _():
                        uc_move(q).wait_send()

                    @pl.when(jnp.logical_not(direct))
                    def _():
                        uc_move(q).wait_recv()

                    cols = pl.ds(pl.multiple_of(q * chunk, chunk), chunk)
                    emitted = jnp.dot(hot0_ref[...], emit_ref[:, cols], preferred_element_type=jnp.float32)
                    for src in range(8):
                        value = one(dec(ug[q, src])) * emitted[src * seqs:(src + 1) * seqs]
                        p_buf[src // 2, src % 2] = value
                    g0[:, cols] = p_buf[...].reshape(8 * seqs, chunk).astype(jnp.bfloat16)

            return carry

        steps = count + 4 * LAG
        if ti == 0:
            steps += GAP + GAP2
        lax.fori_loop(0, steps, body, 0)
        if ti == 0:
            def sent(n, carry):
                h = n % 2
                for yy in range(2):
                    mine = (yy == y) & (2 * r + h == c)

                    @pl.when(jnp.logical_not(mine))
                    def _():
                        u_move(n, yy, 2 * r + h, n // 2).wait_send()
                return carry

            lax.fori_loop(0, count, sent, 0)

    def z_move(time, d):
        return remote(zs.at[time], zr.at[time, d], zr_sem.at[0, time, d], zr_sem.at[1, time, d], lax.rem(r + d, 4), c)

    def z_start(time):
        zs[time] = jnp.broadcast_to(jnp.sum(zacc[time], axis=1, keepdims=True), zs.shape[1:])
        for d in range(1, 4):
            z_move(time, d).start()

    run(0, g1, TICKS1(tick1a, tick1b, tick1c, tick1d))
    z_start(1)
    run(1, g0, TICKS0(tick0a, tick0b))
    z_start(0)
    gw_ref[1] = g1[:, :, :128].reshape(8 * seqs, 128)
    gw_ref[0] = g0[:, :128]
    for time in (1, 0):
        for d in range(1, 4):
            z_move(time, d).wait()
        zr[time, 0] = zs[time]

        def arrived(i):
            return zr[time, lax.rem(r + 4 - i, 4)]

        zc[time] = (arrived(0) + arrived(1)) + (arrived(2) + arrived(3))

    def zc_move(d):
        return remote(zc, zall_ref.at[c], zc_sem.at[0, d], zc_sem.at[1, d], r, lax.rem(c + d, 8))

    for d in range(1, 8):
        zc_move(d).start()
    zall_ref[c] = zc[...]
    fx_move(0, 1, c).wait_send()
    for d in range(4):
        fx_each(d, lambda move: move.wait_send())
    for src in range(4):
        fx_move(1 + src, 0, 2 * src + x).wait_recv()
    for kind in range(3):
        for d in (1, 2, 3):
            fz_sent(kind, d)
    for kind in (1, 2):
        fz_got(kind, 3)
    for d in range(1, 8):
        zc_move(d).wait()


LAG = 2
GAP = 3
GAP2 = 2


def TICKS1(a, b, c, d):
    return ((3, a), (10, b), (16, c), (21, d))


def TICKS0(a, b):
    return ((1, a), (6, b))


def big_call(hot1, hot0, emission, last, forward, transition):
    rows, depth = transition.shape
    seqs = forward.shape[1]
    chunk = CHUNK
    count = rows // chunk
    total = 8 * seqs
    i16, f32, bf16 = jnp.int16, jnp.float32, jnp.bfloat16
    lo1, hi1 = depth * A_MIN * E_MIN * B_MIN, H * A_MAX * E_MAX * B_MAX
    lo0, hi0 = depth * A_MIN * E_MIN * (H * A_MIN * E_MIN * B_MIN), H * A_MAX * E_MAX * hi1
    codes = (code_range(lo1, hi1), code_range(lo0, hi0))
    dma = pltpu.SemaphoreType.DMA
    vmem = pl.BlockSpec(memory_space=pltpu.VMEM)
    anyw = pl.BlockSpec(memory_space=pl.ANY)
    return pl.pallas_call(
        functools.partial(big_kernel, codes),
        out_shape=(
            jax.ShapeDtypeStruct((2, seqs, rows), f32),
            jax.ShapeDtypeStruct((8, 2, seqs, 128), f32),
            jax.ShapeDtypeStruct((2, total, 128), bf16),
            jax.ShapeDtypeStruct((2, 8, 2 * seqs, rows // 2), bf16),
        ),
        in_specs=[vmem] * 5 + [anyw],
        out_specs=(vmem, vmem, vmem, vmem),
        scratch_shapes=[
            pltpu.VMEM((SLOTS, chunk, depth), bf16),
            pltpu.VMEM((4, 2, seqs, chunk), f32),
            pltpu.VMEM((4 * LAG + 1, 4, seqs, chunk), f32),
            pltpu.VMEM((4, 2 * seqs, depth), bf16),
            pltpu.VMEM((total, depth), bf16),
            pltpu.VMEM((2, seqs, 128), f32),
            pltpu.VMEM((2, seqs, 128), f32),
            pltpu.VMEM((2, 4, seqs, 128), f32),
            pltpu.VMEM((2, seqs, 128), f32),
            pltpu.VMEM((count, 2 * seqs, chunk // 2), i16),
            pltpu.VMEM((count // 2, 8, 2 * seqs, chunk // 2), i16),
            pltpu.VMEM((2, count, 4 * seqs, chunk), i16),
            pltpu.VMEM((2, count, 4 * seqs, chunk), i16),
            pltpu.VMEM((2, count, 6 * seqs, chunk // 2), i16),
            pltpu.VMEM((2, count, 6 * seqs, chunk // 2), i16),
            pltpu.VMEM((2, count, 2 * seqs, chunk), i16),
            pltpu.VMEM((2, count, 2 * seqs, chunk), i16),
            pltpu.VMEM((2, count, 2 * seqs, chunk // 2), i16),
            pltpu.VMEM((2, count, 2 * seqs, chunk // 2), i16),
            dma((SLOTS,)),
            dma((2, 2, count)),
            dma((2, 2, count)),
            dma((2, 2, count)),
            dma((2, 2, count)),
            dma((2, 4)),
            dma((2, 4)),
            dma((2, 4)),
            dma((2, count)),
            dma((count // 2, 8)),
            dma((2, count // 2)),
            dma((2, 2, 4)),
            dma((2, 8)),
            dma((2, 5)),
            dma((2, 2, 3, 4)),
        ],
        cost_estimate=pl.CostEstimate(flops=4 * total * rows * depth, bytes_accessed=4 * rows * depth, transcendentals=0),
        compiler_params=pltpu.CompilerParams(collective_id=0, has_side_effects=True, vmem_limit_bytes=60 << 20),
    )(hot1, hot0, emission, last, forward, transition)


def final_kernel(fall_ref, zall_ref, gw_ref, win_ref, u_ref, back_ref, count_ref):
    seqs = u_ref.shape[1]
    c = lax.axis_index("col")

    def work(h):
        totals = None
        for time in (1, 0):
            parts = []
            for src in range(8):
                value = fall_ref[time, src].astype(jnp.float32)[h * seqs:(h + 1) * seqs]
                parts.append(value * (1.0 / zall_ref[src, time, :, :1]))
            weight = jnp.concatenate(parts, axis=0).astype(jnp.bfloat16)
            term = lax.dot_general(weight, gw_ref[time], (((0,), (0,)), ((), ())), preferred_element_type=jnp.float32)
            totals = term if totals is None else totals + term
        count_ref[...] = win_ref[...].astype(jnp.float32) * totals * (H * H / N)

    half = pl.program_id(1)
    for h in range(2):
        pl.when(half == h)(functools.partial(work, h))
    for time in range(2):
        back_ref[time] = u_ref[time] * (1.0 / zall_ref[c, time, :, :1])


def final_call(forward_all, zall, picked, transition, u):
    rows = transition.shape[0]
    seqs = u.shape[1]
    block = 512
    tiles = rows // 2 // block
    return pl.pallas_call(
        final_kernel,
        grid=(tiles, 2),
        in_specs=[
            pl.BlockSpec((2, 8, 2 * seqs, block), lambda j, h: (0, 0, 0, j)),
            pl.BlockSpec(zall.shape, lambda j, h: (0, 0, 0, 0)),
            pl.BlockSpec(picked.shape, lambda j, h: (0, 0, 0)),
            pl.BlockSpec((block, DW), lambda j, h: (h * tiles + j, 0)),
            pl.BlockSpec((2, seqs, block), lambda j, h: (0, 0, h * tiles + j)),
        ],
        out_specs=[
            pl.BlockSpec((2, seqs, block), lambda j, h: (0, 0, h * tiles + j)),
            pl.BlockSpec((block, DW), lambda j, h: (h * tiles + j, 0)),
        ],
        out_shape=[
            jax.ShapeDtypeStruct(u.shape, jnp.float32),
            jax.ShapeDtypeStruct((rows, DW), jnp.float32),
        ],
    )(forward_all, zall, picked, transition, u)


def fast_device(transition, emission, token_ids, forward, backward_last):
    row_index = lax.axis_index("row")
    row_seqs = backward_last.shape[0]
    seqs = forward.shape[1]
    tokens = lax.dynamic_slice_in_dim(token_ids[1], row_index * row_seqs, row_seqs, 0)
    hot1 = (tokens[:, None] == lax.broadcasted_iota(jnp.int32, (row_seqs, emission.shape[0]), 1)).astype(jnp.bfloat16)
    hot0 = (token_ids[0][:, None] == lax.broadcasted_iota(jnp.int32, (8 * seqs, emission.shape[0]), 1)).astype(jnp.bfloat16)
    u, zall, picked, forward_all = big_call(hot1, hot0, emission, backward_last, forward, transition)
    backward, counts = final_call(forward_all, zall, picked, transition, u)
    return (backward, counts)


def in_order(arrived, index):
    count = len(arrived)
    turned = jnp.stack([arrived[-i % count] for i in range(count)] * 2)
    return lax.dynamic_slice_in_dim(turned, (count - index) % count, count, 0)


def gather_small(value, col_count, col_index):
    arrived = [value]
    for k in range(1, col_count):
        arrived.append(lax.ppermute(value, "col", [(c, (c + k) % col_count) for c in range(col_count)]))
    place = lax.broadcasted_iota(jnp.int32, (col_count,) + value.shape, 0)
    out = jnp.zeros(place.shape, value.dtype)
    for k, got in enumerate(arrived):
        out = jnp.where(place == (col_index - k + col_count) % col_count, got[None], out)
    return out


def gather_rows(value, row_count, row_index):
    half = row_count // 2
    arrived = [value]
    for k in range(1, half):
        arrived.append(lax.ppermute(value, "row", [(r, (r + 2 * k) % row_count) for r in range(row_count)]))
    own = in_order(arrived, row_index // 2) if half > 1 else value[None]
    got = lax.ppermute(own, "row", [(r, r ^ 1) for r in range(row_count)])
    even = row_index % 2 == 0
    both = jnp.stack([jnp.where(even, own, got), jnp.where(even, got, own)], axis=1)
    return both.reshape(row_count * value.shape[0], value.shape[1])


def split_pair(partial, scale, col_count, col_index, local_seqs):
    scaled = (partial * scale).reshape(col_count // 2, 2, local_seqs, partial.shape[1])
    side = col_index % 2
    away = lax.dynamic_index_in_dim(scaled, 1 - side, 1, keepdims=False).astype(jnp.float16)
    return away, lax.dynamic_index_in_dim(scaled, side, 1, keepdims=False)


def reduce_scatter(away, keep, col_count, col_index):
    half = col_count // 2
    got = lax.ppermute(away, "col", [(c, c ^ 1) for c in range(col_count)])
    pair = keep + got.astype(jnp.float32)
    here = col_index // 2
    total = lax.dynamic_index_in_dim(pair, here, 0, keepdims=False)
    packed = pair.astype(jnp.float16)
    for k in range(1, half):
        piece = lax.dynamic_index_in_dim(packed, (here + k) % half, 0, keepdims=False)
        got = lax.ppermute(piece, "col", [(c, (c + 2 * k) % col_count) for c in range(col_count)])
        total = total + got.astype(jnp.float32)
    return total


def plain_product(weighted_back, transition, scale, scale_mine, col_count, col_index, local_seqs):
    chunk = transition.shape[0] // CHUNKS
    pieces = []
    for k in range(CHUNKS):
        rows = slice(k * chunk, (k + 1) * chunk)
        partial = lax.dot_general(
            weighted_back, transition[rows], (((1,), (1,)), ((), ())), preferred_element_type=jnp.float32
        )
        away, keep = split_pair(partial, scale, col_count, col_index, local_seqs)
        if k < CHUNKS - 1:
            weighted_back, away = lax.optimization_barrier((weighted_back, away))
        pieces.append(reduce_scatter(away, keep, col_count, col_index))
    return jnp.concatenate(pieces, axis=1) / scale_mine


def on_device(transition, emission, token_ids, forward, backward_last):
    row_count = lax.axis_size("row")
    col_count = lax.axis_size("col")
    row_index = lax.axis_index("row")
    col_index = lax.axis_index("col")
    ratio = col_count // row_count
    local_seqs = forward.shape[1]
    row_seqs = backward_last.shape[0]
    block_src = transition.shape[0]
    block_dst = transition.shape[1]
    seq_total = local_seqs * col_count
    columns = lax.broadcasted_iota(jnp.int32, (row_seqs, emission.shape[0]), 1)
    window = transition[:, :DW]
    outputs = [None, None]
    normals = [None, None]
    picked = [None, None]
    beta = backward_last
    scale = jnp.full((seq_total, 1), 64.0, jnp.float32)
    scale_mine = jnp.full((local_seqs, 1), 64.0, jnp.float32)
    for step in (1, 0):
        tokens = lax.dynamic_slice_in_dim(token_ids[step], row_index * row_seqs, row_seqs, 0)
        onehot = (tokens[:, None] == columns).astype(jnp.bfloat16)
        emitted = jnp.dot(onehot, emission, preferred_element_type=jnp.float32)
        local_back = (emitted * beta).astype(jnp.bfloat16)
        weighted_back = gather_rows(local_back, row_count, row_index)
        picked[step] = weighted_back[:, :DW]
        if step == 1:
            forward_all = lax.all_gather(forward, "col", axis=1, tiled=True)
        mine = plain_product(weighted_back, transition, scale, scale_mine, col_count, col_index, local_seqs)
        norm = jnp.sum(forward[step].astype(jnp.float32) * mine, axis=1)
        sums = lax.psum(jnp.stack([norm, jnp.sum(mine, axis=1)]), "row")
        sums_all = gather_small(sums, col_count, col_index)
        normals[step] = sums_all[:, 0].reshape(seq_total)
        outputs[step] = mine / sums[0][:, None]
        if step == 1:
            halves = outputs[step].reshape(local_seqs, ratio, block_dst)
            arrived = []
            for p in range(ratio):
                part = lax.dynamic_index_in_dim(halves, (col_index + p) % ratio, 1, keepdims=False)
                moves = []
                for r in range(row_count):
                    for c in range(col_count):
                        moves.append((r * col_count + c, (c // ratio) * col_count + r * ratio + (c + p) % ratio))
                arrived.append(lax.ppermute(part, ("row", "col"), moves))
            beta = in_order(arrived, col_index % ratio).reshape(row_seqs, block_dst)
            scale = (16777216.0 * sums_all[:, 0] / sums_all[:, 1]).reshape(seq_total, 1)
            scale_mine = (16777216.0 * sums[0] / sums[1])[:, None]
    totals = jnp.zeros((block_src, DW), jnp.float32)
    for step in (1, 0):
        scaled = (forward_all[step].astype(jnp.float32) / normals[step][:, None]).astype(jnp.bfloat16)
        totals = totals + lax.dot_general(
            scaled, picked[step], (((0,), (0,)), ((), ())), preferred_element_type=jnp.float32
        )
    counts = window.astype(jnp.float32) * totals * (H * H / N)
    return (jnp.stack(outputs), counts)


def solution(mesh):
    in_specs = (P("row", "col"), P(None, "col"), P(), P(None, "col", "row"), P("row", "col"))
    out_specs = (P(None, "col", "row"), P("row", "col"))
    fits = mesh.shape["row"] == 4 and mesh.shape["col"] == 8
    return jax.shard_map(
        fast_device if fits else on_device, mesh=mesh, in_specs=in_specs, out_specs=out_specs, check_vma=False
    )
```

```python
import functools
import math

import jax
import jax.numpy as jnp
from jax import lax
from jax.experimental import pallas as pl
from jax.experimental.pallas import tpu as pltpu
from jax.sharding import PartitionSpec as P

H = 32768
N = 192
DW = 128
CHUNKS = 2
A_MIN, A_MAX = 1.5258789e-06, 0.0024414062
E_MIN, E_MAX = 0.0099487305, 1.0
B_MIN, B_MAX = 0.1, 10.0
CHUNK = 512
SLOTS = 4
MESH = pl.DeviceIdType.MESH


def code_range(lo, hi):
    low = math.log2(lo) - 0.5
    high = math.log2(hi) + 0.5
    return 65000.0 / (high - low), (high + low) / 2


def encode(value, slope, middle):
    return jnp.round(jnp.log2(value) * slope - slope * middle).astype(jnp.int32).astype(jnp.int16)


def decode(code, slope, middle):
    return jnp.exp2(code.astype(jnp.int32).astype(jnp.float32) * (1.0 / slope) + middle)


def big_kernel(
    codes, hot1_ref, hot0_ref, emit_ref, last_ref, fwd_ref, a_ref,
    u_ref, zall_ref, gw_ref, fall_ref,
    a_buf, p_buf, q_buf, g1, g0, zacc, zs, zr, zc, us, ug,
    xs, xr, as_, ar, bs, br, cs, cr,
    a_sem, x_sem, al_sem, b_sem, c_sem, gy_sem, gc_sem, gd_sem, us_sem, ug_sem, uc_sem, zr_sem, zc_sem, fx_sem, fz_sem,
):
    count = xs.shape[1]
    slots, chunk = a_buf.shape[0], a_buf.shape[1]
    seqs = q_buf.shape[2]
    half = chunk // 2
    per = count // 2
    deep = q_buf.shape[0]
    r = lax.axis_index("row")
    c = lax.axis_index("col")
    y, k, z, x = r // 2, r % 2, c // 2, c % 2
    side = z // 2
    outer = (z == 0) | (z == 3)
    z_in, z_out = 1 + side, 3 * side
    z_in2, z_out2 = 2 - side, 3 - 3 * side
    px = 2 * z + 1 - x
    r1, r2 = r + 1 - 2 * k, (r + 2) % 4
    part_cols = g1.shape[2] // 4

    def remote(src, dst, send, recv, row, col):
        return pltpu.make_async_remote_copy(
            src_ref=src, dst_ref=dst, send_sem=send, recv_sem=recv,
            device_id={"row": row, "col": col}, device_id_type=MESH,
        )

    def load(g):
        slot = lax.rem(g, slots)
        n = lax.rem(g, count)
        at = pl.ds(pl.multiple_of(((n % 2) * per + n // 2) * chunk, chunk), chunk)
        return pltpu.make_async_copy(a_ref.at[at], a_buf.at[slot], a_sem.at[slot])

    for g in range(slots):
        load(g).start()
    barrier = pltpu.get_barrier_semaphore()
    me = r * 8 + c

    def greet(i, carry):
        @pl.when(i != me)
        def _():
            pl.semaphore_signal(barrier, inc=1, device_id={"row": i // 8, "col": i % 8}, device_id_type=MESH)
        return carry

    lax.fori_loop(0, 32, greet, 0)

    for j in range(4):
        cols = slice(j * part_cols, (j + 1) * part_cols)
        emitted = jnp.dot(hot1_ref[...], emit_ref[:, cols], preferred_element_type=jnp.float32)
        g1[r, :, cols] = (emitted * last_ref[:, cols]).astype(jnp.bfloat16)
    wide = fall_ref.shape[3]
    for time in range(2):
        for j in range(4):
            left = slice(j * wide // 4, (j + 1) * wide // 4)
            right = slice(wide + j * wide // 4, wide + (j + 1) * wide // 4)
            pair = [fwd_ref[time, :, left].astype(jnp.float32), fwd_ref[time, :, right].astype(jnp.float32)]
            fall_ref[time, c, :, left] = jnp.concatenate(pair, axis=0).astype(jnp.bfloat16)
    pl.semaphore_wait(barrier, 31)

    def g_move(block, j, sem, to):
        at = g1.at[block, :, pl.ds(j * part_cols, part_cols)]
        return remote(at, at, sem.at[0, j], sem.at[1, j], to, c)

    for j in range(4):
        g_move(r, j, gy_sem, r2).start()
        g_move(r, j, gc_sem, r1).start()

    bit = fall_ref.shape[3] // PIECES

    def piece(t, block, p):
        return fall_ref.at[t, block, :, pl.ds(pl.multiple_of(p * bit, bit), bit)]

    def fx_move(i, t, block, p):
        at = piece(t, block, p)
        return remote(at, at, fx_sem.at[0, i, p], fx_sem.at[1, i, p], r, px)

    def fz_move(way, kind, src, to, p):
        t = 0 if kind == 0 else 1
        at = piece(t, 2 * src + (x if kind < 2 else 1 - x), p)
        return remote(at, at, fz_sem.at[0, way, kind, src, p], fz_sem.at[1, way, kind, src, p], r, 2 * to + x)

    def fz_send(kind, d, p, act=lambda move: move.start()):
        @pl.when((z < 3) & (z - d + 1 >= 0))
        def _():
            act(fz_move(0, kind, z - d + 1, z + 1, p))

        @pl.when((z > 0) & (z + d - 1 <= 3))
        def _():
            act(fz_move(1, kind, z + d - 1, z - 1, p))

    def fz_got(kind, d, p):
        @pl.when(z - d >= 0)
        def _():
            fz_move(0, kind, z - d, z, p).wait_recv()

        @pl.when(z + d <= 3)
        def _():
            fz_move(1, kind, z + d, z, p).wait_recv()

    def fx_each(d, act, p):
        @pl.when(z - d >= 0)
        def _():
            act(fx_move(1 + z - d, 0, 2 * (z - d) + x, p))

        if d:
            @pl.when(z + d <= 3)
            def _():
                act(fx_move(1 + z + d, 0, 2 * (z + d) + x, p))

    def start(move):
        move.start()

    def onward(kinds, d, p):
        for kind in kinds:
            if d > 1:
                fz_got(kind, d - 1, p)
            if d < 4:
                fz_send(kind, d, p)

    def pair_lines(p):
        fx_move(0, 1, c, p).wait_recv()
        onward((1, 2), 1, p)

    acts = {
        "pair": lambda p: fx_move(0, 1, c, p).start(), "one1": lambda p: onward((0,), 1, p),
        "one2": lambda p: onward((0,), 2, p), "one3": lambda p: onward((0,), 3, p), "one4": lambda p: onward((0,), 4, p),
        "two1": pair_lines, "two2": lambda p: onward((1, 2), 2, p), "two3": lambda p: onward((1, 2), 3, p),
        "own": lambda p: fx_each(0, start, p), "near": lambda p: fx_each(1, start, p), "mid": lambda p: fx_each(2, start, p),
        "far": lambda p: fx_each(3, start, p),
    }

    def whole(name):
        def body(p, carry):
            acts[name](p)
            return carry

        lax.fori_loop(0, PIECES, body, 0)

    for name in PLAN:
        whole(name)
    for j in range(4):
        g_move(r, j, gy_sem, r2).wait_recv()
        g_move(r2, j, gd_sem, r1).start()
    for j in range(4):
        g_move(r, j, gc_sem, r1).wait()
        g_move(r2, j, gd_sem, r1).wait()
        g_move(r, j, gy_sem, r2).wait_send()

    def two(value):
        return jnp.concatenate([value[:, :half], value[:, half:]], axis=0)

    def one(value):
        n = value.shape[0] // 2
        return jnp.concatenate([value[:n], value[n:]], axis=1)

    zacc[...] = jnp.zeros(zacc.shape, jnp.float32)

    def run(ti, g_buf, ticks):
        time = 1 - ti
        slope, middle = codes[ti]
        enc = functools.partial(encode, slope=slope, middle=middle)
        dec = functools.partial(decode, slope=slope, middle=middle)

        def x_move(n):
            return remote(xs.at[ti, n], xr.at[ti, n], x_sem.at[0, ti, n], x_sem.at[1, ti, n], r, px)

        def a_move(n):
            return remote(as_.at[ti, n], ar.at[ti, n], al_sem.at[0, ti, n], al_sem.at[1, ti, n], r, 2 * z_in + x)

        def b_move(n):
            return remote(bs.at[ti, n], br.at[ti, n], b_sem.at[0, ti, n], b_sem.at[1, ti, n], r, 2 * z_in2 + x)

        def c_move(n):
            return remote(cs.at[ti, n], cr.at[ti, n], c_sem.at[0, ti, n], c_sem.at[1, ti, n], r, 2 * z_out + x)

        def u_move(n, yy, to_col, q):
            return remote(us.at[n], ug.at[q, c], us_sem.at[yy, n], ug_sem.at[q, c], 2 * yy + k, to_col)

        def uc_move(q):
            return remote(ug.at[q], ug.at[q], uc_sem.at[0, q], uc_sem.at[1, q], r1, c)

        def body(m, carry):
            @pl.when(m < count)
            def _():
                g = m + ti * count
                load(g).wait()
                part = lax.dot_general(
                    g_buf[...].reshape(8 * seqs, g_buf.shape[-1]), a_buf[lax.rem(g, slots)], (((1,), (1,)), ((), ())),
                    preferred_element_type=jnp.float32,
                )
                p_buf[...] = part.reshape(p_buf.shape)

                @pl.when(g + slots < 2 * count)
                def _():
                    load(g + slots).start()

                xs[ti, m] = enc(p_buf[:, 1 - x].reshape(4 * seqs, chunk))
                x_move(m).start()
                q_buf[lax.rem(m, deep)] = p_buf[:, x]

            for at, name in ticks:
                pl.when((m >= at) & (m < at + PIECES))(functools.partial(acts[name], m - at))

            @pl.when((m >= LAG) & (m < count + LAG))
            def _():
                n = m - LAG
                s = lax.rem(n, deep)
                x_move(n).wait()
                q_buf[s] += dec(xr[ti, n]).reshape(4, seqs, chunk)

                @pl.when(outer)
                def _():
                    three = jnp.concatenate([q_buf[s, z_in], q_buf[s, z_in2], q_buf[s, z_out2]], axis=0)
                    as_[ti, n] = enc(two(three))
                    a_move(n).start()

            @pl.when((m >= 2 * LAG) & (m < count + 2 * LAG) & jnp.logical_not(outer))
            def _():
                n = m - 2 * LAG
                s = lax.rem(n, deep)
                a_move(n).wait_recv()
                got = one(dec(ar[ti, n]))
                q_buf[s, z_in] += got[:seqs]
                pair = jnp.concatenate([q_buf[s, z_in2] + got[seqs:2 * seqs], q_buf[s, z_out2] + got[2 * seqs:]], axis=0)
                bs[ti, n] = enc(pair)
                b_move(n).start()

            @pl.when((m >= 3 * LAG) & (m < count + 3 * LAG) & jnp.logical_not(outer))
            def _():
                n = m - 3 * LAG
                s = lax.rem(n, deep)
                b_move(n).wait()
                got = dec(br[ti, n])
                q_buf[s, z_in] += got[:seqs]
                cs[ti, n] = enc(two(q_buf[s, z_out] + got[seqs:]))
                c_move(n).start()

            @pl.when((m >= 4 * LAG) & (m < count + 4 * LAG))
            def _():
                n = m - 4 * LAG
                s = lax.rem(n, deep)

                @pl.when(outer)
                def _():
                    c_move(n).wait_recv()
                    a_move(n).wait_send()
                    q_buf[s, z_out] += one(dec(cr[ti, n]))

                @pl.when(jnp.logical_not(outer))
                def _():
                    c_move(n).wait_send()

                value = q_buf[s, z]
                cols = pl.ds(pl.multiple_of(((n % 2) * per + n // 2) * chunk, chunk), chunk)
                u_ref[time, :, cols] = value
                weighed = fwd_ref[time, :, cols].astype(jnp.float32) * value
                total = zacc[time]
                for i in range(chunk // 128):
                    total = total + weighed[:, i * 128:(i + 1) * 128]
                zacc[time] = total
                if ti == 0:
                    h = n % 2
                    q = n // 2
                    to_col = 2 * r + h
                    us[n] = enc(two(value))
                    for yy in range(2):
                        mine = (yy == y) & (to_col == c)

                        @pl.when(mine)
                        def _():
                            ug[q, c] = us[n]

                        @pl.when(jnp.logical_not(mine))
                        def _():
                            u_move(n, yy, to_col, q).start()

            if ti == 0:
                ahead = m - (4 * LAG + GAP + x)
                direct = k == z % 2

                @pl.when((ahead >= 0) & (ahead < 2 * per) & (ahead % 2 == 0) & direct)
                def _():
                    q = ahead // 2
                    for src in range(8):
                        @pl.when(jnp.logical_not((r == z) & (c == src)))
                        def _():
                            remote(us.at[0], ug.at[q, src], us_sem.at[0, 0], ug_sem.at[q, src], r, src).wait_recv()
                    uc_move(q).start()

                later = ahead - GAP2

                @pl.when((later >= 0) & (later < 2 * per) & (later % 2 == 0))
                def _():
                    q = later // 2

                    @pl.when(direct)
                    def _():
                        uc_move(q).wait_send()

                    @pl.when(jnp.logical_not(direct))
                    def _():
                        uc_move(q).wait_recv()

                    cols = pl.ds(pl.multiple_of(q * chunk, chunk), chunk)
                    emitted = jnp.dot(hot0_ref[...], emit_ref[:, cols], preferred_element_type=jnp.float32)
                    for src in range(8):
                        value = one(dec(ug[q, src])) * emitted[src * seqs:(src + 1) * seqs]
                        p_buf[src // 2, src % 2] = value
                    g0[:, cols] = p_buf[...].reshape(8 * seqs, chunk).astype(jnp.bfloat16)

            return carry

        steps = count + 4 * LAG
        if ti == 0:
            steps += GAP + GAP2
        lax.fori_loop(0, steps, body, 0)
        if ti == 0:
            def sent(n, carry):
                h = n % 2
                for yy in range(2):
                    mine = (yy == y) & (2 * r + h == c)

                    @pl.when(jnp.logical_not(mine))
                    def _():
                        u_move(n, yy, 2 * r + h, n // 2).wait_send()
                return carry

            lax.fori_loop(0, count, sent, 0)

    def z_move(time, d):
        return remote(zs.at[time], zr.at[time, d], zr_sem.at[0, time, d], zr_sem.at[1, time, d], lax.rem(r + d, 4), c)

    def z_start(time):
        zs[time] = jnp.broadcast_to(jnp.sum(zacc[time], axis=1, keepdims=True), zs.shape[1:])
        for d in range(1, 4):
            z_move(time, d).start()

    run(0, g1, PLAN1)
    z_start(1)
    run(1, g0, PLAN0)
    z_start(0)
    gw_ref[1] = g1[:, :, :128].reshape(8 * seqs, 128)
    gw_ref[0] = g0[:, :128]
    def zc_move(time, d):
        return remote(zc.at[time], zall_ref.at[c, time], zc_sem.at[0, time, d], zc_sem.at[1, time, d], r, lax.rem(c + d, 8))

    def z_spread(time):
        for d in range(1, 4):
            z_move(time, d).wait()
        zr[time, 0] = zs[time]

        def arrived(i):
            return zr[time, lax.rem(r + 4 - i, 4)]

        zc[time] = (arrived(0) + arrived(1)) + (arrived(2) + arrived(3))
        zall_ref[c, time] = zc[time]
        for d in range(1, 8):
            zc_move(time, d).start()

    z_spread(1)
    z_spread(0)
    def finish(p, carry):
        for kind in (1, 2):
            fz_got(kind, 3, p)
        for kind in range(3):
            for d in (1, 2, 3):
                fz_send(kind, d, p, lambda move: move.wait_send())
        fx_move(0, 1, c, p).wait_send()
        for d in range(4):
            fx_each(d, lambda move: move.wait_send(), p)
        for src in range(4):
            fx_move(1 + src, 0, 2 * src + x, p).wait_recv()
        return carry

    lax.fori_loop(0, PIECES, finish, 0)
    for time in range(2):
        for d in range(1, 8):
            zc_move(time, d).wait()


LAG = 2
GAP = 3
GAP2 = 2


PIECES = 8
PLAN = ("pair", "one1")
PLAN1 = ((1, "one2"), (8, "one3"), (14, "two1"), (14, "own"))
PLAN0 = ((0, "one4"), (0, "two2"), (8, "near"), (8, "two3"), (16, "mid"), (16, "far"))


def big_call(hot1, hot0, emission, last, forward, transition):
    rows, depth = transition.shape
    seqs = forward.shape[1]
    chunk = CHUNK
    count = rows // chunk
    total = 8 * seqs
    i16, f32, bf16 = jnp.int16, jnp.float32, jnp.bfloat16
    lo1, hi1 = depth * A_MIN * E_MIN * B_MIN, H * A_MAX * E_MAX * B_MAX
    lo0, hi0 = depth * A_MIN * E_MIN * (H * A_MIN * E_MIN * B_MIN), H * A_MAX * E_MAX * hi1
    codes = (code_range(lo1, hi1), code_range(lo0, hi0))
    dma = pltpu.SemaphoreType.DMA
    vmem = pl.BlockSpec(memory_space=pltpu.VMEM)
    anyw = pl.BlockSpec(memory_space=pl.ANY)
    return pl.pallas_call(
        functools.partial(big_kernel, codes),
        out_shape=(
            jax.ShapeDtypeStruct((2, seqs, rows), f32),
            jax.ShapeDtypeStruct((8, 2, seqs, 128), f32),
            jax.ShapeDtypeStruct((2, total, 128), bf16),
            jax.ShapeDtypeStruct((2, 8, 2 * seqs, rows // 2), bf16),
        ),
        in_specs=[vmem] * 5 + [anyw],
        out_specs=(vmem, vmem, vmem, vmem),
        scratch_shapes=[
            pltpu.VMEM((SLOTS, chunk, depth), bf16),
            pltpu.VMEM((4, 2, seqs, chunk), f32),
            pltpu.VMEM((4 * LAG + 1, 4, seqs, chunk), f32),
            pltpu.VMEM((4, 2 * seqs, depth), bf16),
            pltpu.VMEM((total, depth), bf16),
            pltpu.VMEM((2, seqs, 128), f32),
            pltpu.VMEM((2, seqs, 128), f32),
            pltpu.VMEM((2, 4, seqs, 128), f32),
            pltpu.VMEM((2, seqs, 128), f32),
            pltpu.VMEM((count, 2 * seqs, chunk // 2), i16),
            pltpu.VMEM((count // 2, 8, 2 * seqs, chunk // 2), i16),
            pltpu.VMEM((2, count, 4 * seqs, chunk), i16),
            pltpu.VMEM((2, count, 4 * seqs, chunk), i16),
            pltpu.VMEM((2, count, 6 * seqs, chunk // 2), i16),
            pltpu.VMEM((2, count, 6 * seqs, chunk // 2), i16),
            pltpu.VMEM((2, count, 2 * seqs, chunk), i16),
            pltpu.VMEM((2, count, 2 * seqs, chunk), i16),
            pltpu.VMEM((2, count, 2 * seqs, chunk // 2), i16),
            pltpu.VMEM((2, count, 2 * seqs, chunk // 2), i16),
            dma((SLOTS,)),
            dma((2, 2, count)),
            dma((2, 2, count)),
            dma((2, 2, count)),
            dma((2, 2, count)),
            dma((2, 4)),
            dma((2, 4)),
            dma((2, 4)),
            dma((2, count)),
            dma((count // 2, 8)),
            dma((2, count // 2)),
            dma((2, 2, 4)),
            dma((2, 2, 8)),
            dma((2, 5, PIECES)),
            dma((2, 2, 3, 4, PIECES)),
        ],
        cost_estimate=pl.CostEstimate(flops=4 * total * rows * depth, bytes_accessed=4 * rows * depth, transcendentals=0),
        compiler_params=pltpu.CompilerParams(collective_id=0, has_side_effects=True, vmem_limit_bytes=60 << 20),
    )(hot1, hot0, emission, last, forward, transition)


def final_kernel(fall_ref, zall_ref, gw_ref, win_ref, u_ref, back_ref, count_ref):
    seqs = u_ref.shape[1]
    c = lax.axis_index("col")

    def work(h):
        parts = []
        for time in range(2):
            for src in range(8):
                value = fall_ref[time, src].astype(jnp.float32)[h * seqs:(h + 1) * seqs]
                parts.append(value * (1.0 / zall_ref[src, time, :, :1]))
        weight = jnp.concatenate(parts, axis=0).astype(jnp.bfloat16)
        totals = jnp.dot(gw_ref[...], weight, preferred_element_type=jnp.float32).T
        count_ref[...] = win_ref[...].astype(jnp.float32) * totals * (H * H / N)

    half = pl.program_id(1)
    for h in range(2):
        pl.when(half == h)(functools.partial(work, h))
    for time in range(2):
        back_ref[time] = u_ref[time] * (1.0 / zall_ref[c, time, :, :1])


def final_call(forward_all, zall, picked, transition, u):
    rows = transition.shape[0]
    seqs = u.shape[1]
    block = 2048
    tiles = rows // 2 // block
    return pl.pallas_call(
        final_kernel,
        grid=(tiles, 2),
        in_specs=[
            pl.BlockSpec((2, 8, 2 * seqs, block), lambda j, h: (0, 0, 0, j)),
            pl.BlockSpec(zall.shape, lambda j, h: (0, 0, 0, 0)),
            pl.BlockSpec(picked.shape, lambda j, h: (0, 0)),
            pl.BlockSpec((block, DW), lambda j, h: (h * tiles + j, 0)),
            pl.BlockSpec((2, seqs, block), lambda j, h: (0, 0, h * tiles + j)),
        ],
        out_specs=[
            pl.BlockSpec((2, seqs, block), lambda j, h: (0, 0, h * tiles + j)),
            pl.BlockSpec((block, DW), lambda j, h: (h * tiles + j, 0)),
        ],
        out_shape=[
            jax.ShapeDtypeStruct(u.shape, jnp.float32),
            jax.ShapeDtypeStruct((rows, DW), jnp.float32),
        ],
    )(forward_all, zall, picked, transition, u)


def fast_device(transition, emission, token_ids, forward, backward_last):
    row_index = lax.axis_index("row")
    row_seqs = backward_last.shape[0]
    seqs = forward.shape[1]
    tokens = lax.dynamic_slice_in_dim(token_ids[1], row_index * row_seqs, row_seqs, 0)
    hot1 = (tokens[:, None] == lax.broadcasted_iota(jnp.int32, (row_seqs, emission.shape[0]), 1)).astype(jnp.bfloat16)
    hot0 = (token_ids[0][:, None] == lax.broadcasted_iota(jnp.int32, (8 * seqs, emission.shape[0]), 1)).astype(jnp.bfloat16)
    u, zall, picked, forward_all = big_call(hot1, hot0, emission, backward_last, forward, transition)
    backward, counts = final_call(forward_all, zall, picked.reshape(16 * seqs, DW).T, transition, u)
    return (backward, counts)


def in_order(arrived, index):
    count = len(arrived)
    turned = jnp.stack([arrived[-i % count] for i in range(count)] * 2)
    return lax.dynamic_slice_in_dim(turned, (count - index) % count, count, 0)


def gather_small(value, col_count, col_index):
    arrived = [value]
    for k in range(1, col_count):
        arrived.append(lax.ppermute(value, "col", [(c, (c + k) % col_count) for c in range(col_count)]))
    place = lax.broadcasted_iota(jnp.int32, (col_count,) + value.shape, 0)
    out = jnp.zeros(place.shape, value.dtype)
    for k, got in enumerate(arrived):
        out = jnp.where(place == (col_index - k + col_count) % col_count, got[None], out)
    return out


def gather_rows(value, row_count, row_index):
    half = row_count // 2
    arrived = [value]
    for k in range(1, half):
        arrived.append(lax.ppermute(value, "row", [(r, (r + 2 * k) % row_count) for r in range(row_count)]))
    own = in_order(arrived, row_index // 2) if half > 1 else value[None]
    got = lax.ppermute(own, "row", [(r, r ^ 1) for r in range(row_count)])
    even = row_index % 2 == 0
    both = jnp.stack([jnp.where(even, own, got), jnp.where(even, got, own)], axis=1)
    return both.reshape(row_count * value.shape[0], value.shape[1])


def split_pair(partial, scale, col_count, col_index, local_seqs):
    scaled = (partial * scale).reshape(col_count // 2, 2, local_seqs, partial.shape[1])
    side = col_index % 2
    away = lax.dynamic_index_in_dim(scaled, 1 - side, 1, keepdims=False).astype(jnp.float16)
    return away, lax.dynamic_index_in_dim(scaled, side, 1, keepdims=False)


def reduce_scatter(away, keep, col_count, col_index):
    half = col_count // 2
    got = lax.ppermute(away, "col", [(c, c ^ 1) for c in range(col_count)])
    pair = keep + got.astype(jnp.float32)
    here = col_index // 2
    total = lax.dynamic_index_in_dim(pair, here, 0, keepdims=False)
    packed = pair.astype(jnp.float16)
    for k in range(1, half):
        piece = lax.dynamic_index_in_dim(packed, (here + k) % half, 0, keepdims=False)
        got = lax.ppermute(piece, "col", [(c, (c + 2 * k) % col_count) for c in range(col_count)])
        total = total + got.astype(jnp.float32)
    return total


def plain_product(weighted_back, transition, scale, scale_mine, col_count, col_index, local_seqs):
    chunk = transition.shape[0] // CHUNKS
    pieces = []
    for k in range(CHUNKS):
        rows = slice(k * chunk, (k + 1) * chunk)
        partial = lax.dot_general(
            weighted_back, transition[rows], (((1,), (1,)), ((), ())), preferred_element_type=jnp.float32
        )
        away, keep = split_pair(partial, scale, col_count, col_index, local_seqs)
        if k < CHUNKS - 1:
            weighted_back, away = lax.optimization_barrier((weighted_back, away))
        pieces.append(reduce_scatter(away, keep, col_count, col_index))
    return jnp.concatenate(pieces, axis=1) / scale_mine


def on_device(transition, emission, token_ids, forward, backward_last):
    row_count = lax.axis_size("row")
    col_count = lax.axis_size("col")
    row_index = lax.axis_index("row")
    col_index = lax.axis_index("col")
    ratio = col_count // row_count
    local_seqs = forward.shape[1]
    row_seqs = backward_last.shape[0]
    block_src = transition.shape[0]
    block_dst = transition.shape[1]
    seq_total = local_seqs * col_count
    columns = lax.broadcasted_iota(jnp.int32, (row_seqs, emission.shape[0]), 1)
    window = transition[:, :DW]
    outputs = [None, None]
    normals = [None, None]
    picked = [None, None]
    beta = backward_last
    scale = jnp.full((seq_total, 1), 64.0, jnp.float32)
    scale_mine = jnp.full((local_seqs, 1), 64.0, jnp.float32)
    for step in (1, 0):
        tokens = lax.dynamic_slice_in_dim(token_ids[step], row_index * row_seqs, row_seqs, 0)
        onehot = (tokens[:, None] == columns).astype(jnp.bfloat16)
        emitted = jnp.dot(onehot, emission, preferred_element_type=jnp.float32)
        local_back = (emitted * beta).astype(jnp.bfloat16)
        weighted_back = gather_rows(local_back, row_count, row_index)
        picked[step] = weighted_back[:, :DW]
        if step == 1:
            forward_all = lax.all_gather(forward, "col", axis=1, tiled=True)
        mine = plain_product(weighted_back, transition, scale, scale_mine, col_count, col_index, local_seqs)
        norm = jnp.sum(forward[step].astype(jnp.float32) * mine, axis=1)
        sums = lax.psum(jnp.stack([norm, jnp.sum(mine, axis=1)]), "row")
        sums_all = gather_small(sums, col_count, col_index)
        normals[step] = sums_all[:, 0].reshape(seq_total)
        outputs[step] = mine / sums[0][:, None]
        if step == 1:
            halves = outputs[step].reshape(local_seqs, ratio, block_dst)
            arrived = []
            for p in range(ratio):
                part = lax.dynamic_index_in_dim(halves, (col_index + p) % ratio, 1, keepdims=False)
                moves = []
                for r in range(row_count):
                    for c in range(col_count):
                        moves.append((r * col_count + c, (c // ratio) * col_count + r * ratio + (c + p) % ratio))
                arrived.append(lax.ppermute(part, ("row", "col"), moves))
            beta = in_order(arrived, col_index % ratio).reshape(row_seqs, block_dst)
            scale = (16777216.0 * sums_all[:, 0] / sums_all[:, 1]).reshape(seq_total, 1)
            scale_mine = (16777216.0 * sums[0] / sums[1])[:, None]
    totals = jnp.zeros((block_src, DW), jnp.float32)
    for step in (1, 0):
        scaled = (forward_all[step].astype(jnp.float32) / normals[step][:, None]).astype(jnp.bfloat16)
        totals = totals + lax.dot_general(
            scaled, picked[step], (((0,), (0,)), ((), ())), preferred_element_type=jnp.float32
        )
    counts = window.astype(jnp.float32) * totals * (H * H / N)
    return (jnp.stack(outputs), counts)


def solution(mesh):
    in_specs = (P("row", "col"), P(None, "col"), P(), P(None, "col", "row"), P("row", "col"))
    out_specs = (P(None, "col", "row"), P("row", "col"))
    fits = mesh.shape["row"] == 4 and mesh.shape["col"] == 8
    return jax.shard_map(
        fast_device if fits else on_device, mesh=mesh, in_specs=in_specs, out_specs=out_specs, check_vma=False
    )
```

```python
import functools
import math

import jax
import jax.numpy as jnp
from jax import lax
from jax.experimental import pallas as pl
from jax.experimental.pallas import tpu as pltpu
from jax.sharding import PartitionSpec as P

H = 32768
N = 192
DW = 128
CHUNKS = 2
A_MIN, A_MAX = 1.5258789e-06, 0.0024414062
E_MIN, E_MAX = 0.0099487305, 1.0
B_MIN, B_MAX = 0.1, 10.0
CHUNK = 512
SLOTS = 4
MESH = pl.DeviceIdType.MESH


def code_range(lo, hi):
    low = math.log2(lo) - 0.5
    high = math.log2(hi) + 0.5
    return 65000.0 / (high - low), (high + low) / 2


def encode(value, slope, middle):
    return jnp.round(jnp.log2(value) * slope - slope * middle).astype(jnp.int32).astype(jnp.int16)


def decode(code, slope, middle):
    return jnp.exp2(code.astype(jnp.int32).astype(jnp.float32) * (1.0 / slope) + middle)


def big_kernel(
    codes, hot1_ref, hot0_ref, emit_ref, last_ref, fwd_ref, a_ref,
    u_ref, zall_ref, gw_ref, fall_ref,
    a_buf, p_buf, q_buf, g1, g0, zacc, zs, zr, zc, us, ug,
    xs, xr, as_, ar, bs, br, cs, cr,
    a_sem, x_sem, al_sem, b_sem, c_sem, gy_sem, gc_sem, gd_sem, us_sem, ug_sem, uc_sem, zr_sem, zc_sem, fx_sem, fz_sem,
):
    count = xs.shape[1]
    slots, chunk = a_buf.shape[0], a_buf.shape[1]
    seqs = q_buf.shape[2]
    half = chunk // 2
    per = count // 2
    deep = q_buf.shape[0]
    r = lax.axis_index("row")
    c = lax.axis_index("col")
    y, k, z, x = r // 2, r % 2, c // 2, c % 2
    side = z // 2
    outer = (z == 0) | (z == 3)
    z_in, z_out = 1 + side, 3 * side
    z_in2, z_out2 = 2 - side, 3 - 3 * side
    px = 2 * z + 1 - x
    r1, r2 = r + 1 - 2 * k, (r + 2) % 4
    part_cols = g1.shape[2] // 4

    def remote(src, dst, send, recv, row, col):
        return pltpu.make_async_remote_copy(
            src_ref=src, dst_ref=dst, send_sem=send, recv_sem=recv,
            device_id={"row": row, "col": col}, device_id_type=MESH,
        )

    def load(g):
        slot = lax.rem(g, slots)
        n = lax.rem(g, count)
        at = pl.ds(pl.multiple_of(((n % 2) * per + n // 2) * chunk, chunk), chunk)
        return pltpu.make_async_copy(a_ref.at[at], a_buf.at[slot], a_sem.at[slot])

    for g in range(slots):
        load(g).start()
    barrier = pltpu.get_barrier_semaphore()
    me = r * 8 + c

    def greet(i, carry):
        @pl.when(i != me)
        def _():
            pl.semaphore_signal(barrier, inc=1, device_id={"row": i // 8, "col": i % 8}, device_id_type=MESH)
        return carry

    lax.fori_loop(0, 32, greet, 0)

    for j in range(4):
        cols = slice(j * part_cols, (j + 1) * part_cols)
        emitted = jnp.dot(hot1_ref[...], emit_ref[:, cols], preferred_element_type=jnp.float32)
        g1[r, :, cols] = (emitted * last_ref[:, cols]).astype(jnp.bfloat16)
    wide = fall_ref.shape[3]
    for time in range(2):
        for j in range(4):
            left = slice(j * wide // 4, (j + 1) * wide // 4)
            right = slice(wide + j * wide // 4, wide + (j + 1) * wide // 4)
            pair = [fwd_ref[time, :, left].astype(jnp.float32), fwd_ref[time, :, right].astype(jnp.float32)]
            fall_ref[time, c, :, left] = jnp.concatenate(pair, axis=0).astype(jnp.bfloat16)
    pl.semaphore_wait(barrier, 31)

    def g_move(block, j, sem, to):
        at = g1.at[block, :, pl.ds(j * part_cols, part_cols)]
        return remote(at, at, sem.at[0, j], sem.at[1, j], to, c)

    for j in range(4):
        g_move(r, j, gy_sem, r2).start()
        g_move(r, j, gc_sem, r1).start()

    bit = fall_ref.shape[3] // PIECES

    def piece(t, block, p):
        return fall_ref.at[t, block, :, pl.ds(pl.multiple_of(p * bit, bit), bit)]

    def fx_move(i, t, block, p):
        at = piece(t, block, p)
        return remote(at, at, fx_sem.at[0, i, p], fx_sem.at[1, i, p], r, px)

    def fz_move(way, kind, src, to, p):
        t = 0 if kind == 0 else 1
        at = piece(t, 2 * src + (x if kind < 2 else 1 - x), p)
        return remote(at, at, fz_sem.at[0, way, kind, src, p], fz_sem.at[1, way, kind, src, p], r, 2 * to + x)

    def fz_send(kind, d, p, act=lambda move: move.start()):
        @pl.when((z < 3) & (z - d + 1 >= 0))
        def _():
            act(fz_move(0, kind, z - d + 1, z + 1, p))

        @pl.when((z > 0) & (z + d - 1 <= 3))
        def _():
            act(fz_move(1, kind, z + d - 1, z - 1, p))

    def fz_got(kind, d, p):
        @pl.when(z - d >= 0)
        def _():
            fz_move(0, kind, z - d, z, p).wait_recv()

        @pl.when(z + d <= 3)
        def _():
            fz_move(1, kind, z + d, z, p).wait_recv()

    def fx_each(d, act, p):
        @pl.when(z - d >= 0)
        def _():
            act(fx_move(1 + z - d, 0, 2 * (z - d) + x, p))

        if d:
            @pl.when(z + d <= 3)
            def _():
                act(fx_move(1 + z + d, 0, 2 * (z + d) + x, p))

    def start(move):
        move.start()

    def onward(kinds, d, p):
        for kind in kinds:
            if d > 1:
                fz_got(kind, d - 1, p)
            if d < 4:
                fz_send(kind, d, p)

    def pair_lines(p):
        fx_move(0, 1, c, p).wait_recv()
        onward((1, 2), 1, p)

    acts = {
        "pair": lambda p: fx_move(0, 1, c, p).start(), "one1": lambda p: onward((0,), 1, p),
        "one2": lambda p: onward((0,), 2, p), "one3": lambda p: onward((0,), 3, p), "one4": lambda p: onward((0,), 4, p),
        "two1": pair_lines, "two2": lambda p: onward((1, 2), 2, p), "two3": lambda p: onward((1, 2), 3, p),
        "own": lambda p: fx_each(0, start, p), "near": lambda p: fx_each(1, start, p), "mid": lambda p: fx_each(2, start, p),
        "far": lambda p: fx_each(3, start, p),
    }

    def whole(name):
        def body(p, carry):
            acts[name](p)
            return carry

        lax.fori_loop(0, PIECES, body, 0)

    for name in PLAN:
        whole(name)
    for j in range(4):
        g_move(r, j, gy_sem, r2).wait_recv()
        g_move(r2, j, gd_sem, r1).start()
    for j in range(4):
        g_move(r, j, gc_sem, r1).wait()
        g_move(r2, j, gd_sem, r1).wait()
        g_move(r, j, gy_sem, r2).wait_send()

    def two(value):
        return jnp.concatenate([value[:, :half], value[:, half:]], axis=0)

    def one(value):
        n = value.shape[0] // 2
        return jnp.concatenate([value[:n], value[n:]], axis=1)

    zacc[...] = jnp.zeros(zacc.shape, jnp.float32)

    def run(ti, g_buf, ticks):
        time = 1 - ti
        slope, middle = codes[ti]
        enc = functools.partial(encode, slope=slope, middle=middle)
        dec = functools.partial(decode, slope=slope, middle=middle)

        def x_move(n):
            return remote(xs.at[ti, n], xr.at[ti, n], x_sem.at[0, ti, n], x_sem.at[1, ti, n], r, px)

        def a_move(n):
            return remote(as_.at[ti, n], ar.at[ti, n], al_sem.at[0, ti, n], al_sem.at[1, ti, n], r, 2 * z_in + x)

        def b_move(n):
            return remote(bs.at[ti, n], br.at[ti, n], b_sem.at[0, ti, n], b_sem.at[1, ti, n], r, 2 * z_in2 + x)

        def c_move(n):
            return remote(cs.at[ti, n], cr.at[ti, n], c_sem.at[0, ti, n], c_sem.at[1, ti, n], r, 2 * z_out + x)

        def u_move(n, yy, to_col, q):
            return remote(us.at[n], ug.at[q, c], us_sem.at[yy, n], ug_sem.at[q, c], 2 * yy + k, to_col)

        def uc_move(q):
            return remote(ug.at[q], ug.at[q], uc_sem.at[0, q], uc_sem.at[1, q], r1, c)

        def body(m, carry):
            @pl.when(m < count)
            def _():
                g = m + ti * count
                load(g).wait()
                part = lax.dot_general(
                    g_buf[...].reshape(8 * seqs, g_buf.shape[-1]), a_buf[lax.rem(g, slots)], (((1,), (1,)), ((), ())),
                    preferred_element_type=jnp.float32,
                )
                p_buf[...] = part.reshape(p_buf.shape)

                @pl.when(g + slots < 2 * count)
                def _():
                    load(g + slots).start()

                xs[ti, m] = enc(p_buf[:, 1 - x].reshape(4 * seqs, chunk))
                x_move(m).start()
                q_buf[lax.rem(m, deep)] = p_buf[:, x]

            for at, name in ticks:
                pl.when((m >= at) & (m < at + PIECES))(functools.partial(acts[name], m - at))

            @pl.when((m >= LAG) & (m < count + LAG))
            def _():
                n = m - LAG
                s = lax.rem(n, deep)
                x_move(n).wait()
                q_buf[s] += dec(xr[ti, n]).reshape(4, seqs, chunk)

                @pl.when(outer)
                def _():
                    three = jnp.concatenate([q_buf[s, z_in], q_buf[s, z_in2], q_buf[s, z_out2]], axis=0)
                    as_[ti, n] = enc(two(three))
                    a_move(n).start()

            @pl.when((m >= 2 * LAG) & (m < count + 2 * LAG) & jnp.logical_not(outer))
            def _():
                n = m - 2 * LAG
                s = lax.rem(n, deep)
                a_move(n).wait_recv()
                got = one(dec(ar[ti, n]))
                q_buf[s, z_in] += got[:seqs]
                pair = jnp.concatenate([q_buf[s, z_in2] + got[seqs:2 * seqs], q_buf[s, z_out2] + got[2 * seqs:]], axis=0)
                bs[ti, n] = enc(pair)
                b_move(n).start()

            @pl.when((m >= 3 * LAG) & (m < count + 3 * LAG) & jnp.logical_not(outer))
            def _():
                n = m - 3 * LAG
                s = lax.rem(n, deep)
                b_move(n).wait()
                got = dec(br[ti, n])
                q_buf[s, z_in] += got[:seqs]
                cs[ti, n] = enc(two(q_buf[s, z_out] + got[seqs:]))
                c_move(n).start()

            @pl.when((m >= 4 * LAG) & (m < count + 4 * LAG))
            def _():
                n = m - 4 * LAG
                s = lax.rem(n, deep)

                @pl.when(outer)
                def _():
                    c_move(n).wait_recv()
                    a_move(n).wait_send()
                    q_buf[s, z_out] += one(dec(cr[ti, n]))

                @pl.when(jnp.logical_not(outer))
                def _():
                    c_move(n).wait_send()

                value = q_buf[s, z]
                cols = pl.ds(pl.multiple_of(((n % 2) * per + n // 2) * chunk, chunk), chunk)
                u_ref[time, :, cols] = value
                weighed = fwd_ref[time, :, cols].astype(jnp.float32) * value
                total = zacc[time]
                for i in range(chunk // 128):
                    total = total + weighed[:, i * 128:(i + 1) * 128]
                zacc[time] = total
                if ti == 0:
                    h = n % 2
                    q = n // 2
                    to_col = 2 * r + h
                    us[n] = enc(two(value))
                    for yy in range(2):
                        mine = (yy == y) & (to_col == c)

                        @pl.when(mine)
                        def _():
                            ug[q, c] = us[n]

                        @pl.when(jnp.logical_not(mine))
                        def _():
                            u_move(n, yy, to_col, q).start()

            if ti == 0:
                ahead = m - (4 * LAG + GAP + x)
                direct = k == z % 2

                @pl.when((ahead >= 0) & (ahead < 2 * per) & (ahead % 2 == 0) & direct)
                def _():
                    q = ahead // 2
                    for src in range(8):
                        @pl.when(jnp.logical_not((r == z) & (c == src)))
                        def _():
                            remote(us.at[0], ug.at[q, src], us_sem.at[0, 0], ug_sem.at[q, src], r, src).wait_recv()
                    uc_move(q).start()

                later = ahead - GAP2

                @pl.when((later >= 0) & (later < 2 * per) & (later % 2 == 0))
                def _():
                    q = later // 2

                    @pl.when(direct)
                    def _():
                        uc_move(q).wait_send()

                    @pl.when(jnp.logical_not(direct))
                    def _():
                        uc_move(q).wait_recv()

                    cols = pl.ds(pl.multiple_of(q * chunk, chunk), chunk)
                    emitted = jnp.dot(hot0_ref[...], emit_ref[:, cols], preferred_element_type=jnp.float32)
                    for src in range(8):
                        value = one(dec(ug[q, src])) * emitted[src * seqs:(src + 1) * seqs]
                        p_buf[src // 2, src % 2] = value
                    g0[:, cols] = p_buf[...].reshape(8 * seqs, chunk).astype(jnp.bfloat16)

            return carry

        steps = count + 4 * LAG
        if ti == 0:
            steps += GAP + GAP2
        lax.fori_loop(0, steps, body, 0)
        if ti == 0:
            def sent(n, carry):
                h = n % 2
                for yy in range(2):
                    mine = (yy == y) & (2 * r + h == c)

                    @pl.when(jnp.logical_not(mine))
                    def _():
                        u_move(n, yy, 2 * r + h, n // 2).wait_send()
                return carry

            lax.fori_loop(0, count, sent, 0)

    def z_move(time, d):
        return remote(zs.at[time], zr.at[time, d], zr_sem.at[0, time, d], zr_sem.at[1, time, d], lax.rem(r + d, 4), c)

    def z_start(time):
        zs[time] = jnp.broadcast_to(jnp.sum(zacc[time], axis=1, keepdims=True), zs.shape[1:])
        for d in range(1, 4):
            z_move(time, d).start()

    run(0, g1, PLAN1)
    z_start(1)
    run(1, g0, PLAN0)
    z_start(0)
    gw_ref[1] = g1[:, :, :128].reshape(8 * seqs, 128)
    gw_ref[0] = g0[:, :128]
    def zc_move(time, d):
        return remote(zc.at[time], zall_ref.at[c, time], zc_sem.at[0, time, d], zc_sem.at[1, time, d], r, lax.rem(c + d, 8))

    def z_spread(time):
        for d in range(1, 4):
            z_move(time, d).wait()
        zr[time, 0] = zs[time]

        def arrived(i):
            return zr[time, lax.rem(r + 4 - i, 4)]

        zc[time] = (arrived(0) + arrived(1)) + (arrived(2) + arrived(3))
        zall_ref[c, time] = zc[time]
        for d in range(1, 8):
            zc_move(time, d).start()

    z_spread(1)
    z_spread(0)
    def finish(p, carry):
        for kind in (1, 2):
            fz_got(kind, 3, p)
        for kind in range(3):
            for d in (1, 2, 3):
                fz_send(kind, d, p, lambda move: move.wait_send())
        fx_move(0, 1, c, p).wait_send()
        for d in range(4):
            fx_each(d, lambda move: move.wait_send(), p)
        for src in range(4):
            fx_move(1 + src, 0, 2 * src + x, p).wait_recv()
        return carry

    lax.fori_loop(0, PIECES, finish, 0)
    for time in range(2):
        for d in range(1, 8):
            zc_move(time, d).wait()


LAG = 2
GAP = 3
GAP2 = 2


PIECES = 8
PLAN = ("pair", "one1")
PLAN1 = ((0, "one2"), (5, "one3"), (14, "own"))
PLAN0 = ((0, "one4"), (0, "two1"), (8, "two2"), (16, "near"), (16, "two3"), (16, "mid"), (16, "far"))


def big_call(hot1, hot0, emission, last, forward, transition):
    rows, depth = transition.shape
    seqs = forward.shape[1]
    chunk = CHUNK
    count = rows // chunk
    total = 8 * seqs
    i16, f32, bf16 = jnp.int16, jnp.float32, jnp.bfloat16
    lo1, hi1 = depth * A_MIN * E_MIN * B_MIN, H * A_MAX * E_MAX * B_MAX
    lo0, hi0 = depth * A_MIN * E_MIN * (H * A_MIN * E_MIN * B_MIN), H * A_MAX * E_MAX * hi1
    codes = (code_range(lo1, hi1), code_range(lo0, hi0))
    dma = pltpu.SemaphoreType.DMA
    vmem = pl.BlockSpec(memory_space=pltpu.VMEM)
    anyw = pl.BlockSpec(memory_space=pl.ANY)
    return pl.pallas_call(
        functools.partial(big_kernel, codes),
        out_shape=(
            jax.ShapeDtypeStruct((2, seqs, rows), f32),
            jax.ShapeDtypeStruct((8, 2, seqs, 128), f32),
            jax.ShapeDtypeStruct((2, total, 128), bf16),
            jax.ShapeDtypeStruct((2, 8, 2 * seqs, rows // 2), bf16),
        ),
        in_specs=[vmem] * 5 + [anyw],
        out_specs=(vmem, vmem, vmem, vmem),
        scratch_shapes=[
            pltpu.VMEM((SLOTS, chunk, depth), bf16),
            pltpu.VMEM((4, 2, seqs, chunk), f32),
            pltpu.VMEM((4 * LAG + 1, 4, seqs, chunk), f32),
            pltpu.VMEM((4, 2 * seqs, depth), bf16),
            pltpu.VMEM((total, depth), bf16),
            pltpu.VMEM((2, seqs, 128), f32),
            pltpu.VMEM((2, seqs, 128), f32),
            pltpu.VMEM((2, 4, seqs, 128), f32),
            pltpu.VMEM((2, seqs, 128), f32),
            pltpu.VMEM((count, 2 * seqs, chunk // 2), i16),
            pltpu.VMEM((count // 2, 8, 2 * seqs, chunk // 2), i16),
            pltpu.VMEM((2, count, 4 * seqs, chunk), i16),
            pltpu.VMEM((2, count, 4 * seqs, chunk), i16),
            pltpu.VMEM((2, count, 6 * seqs, chunk // 2), i16),
            pltpu.VMEM((2, count, 6 * seqs, chunk // 2), i16),
            pltpu.VMEM((2, count, 2 * seqs, chunk), i16),
            pltpu.VMEM((2, count, 2 * seqs, chunk), i16),
            pltpu.VMEM((2, count, 2 * seqs, chunk // 2), i16),
            pltpu.VMEM((2, count, 2 * seqs, chunk // 2), i16),
            dma((SLOTS,)),
            dma((2, 2, count)),
            dma((2, 2, count)),
            dma((2, 2, count)),
            dma((2, 2, count)),
            dma((2, 4)),
            dma((2, 4)),
            dma((2, 4)),
            dma((2, count)),
            dma((count // 2, 8)),
            dma((2, count // 2)),
            dma((2, 2, 4)),
            dma((2, 2, 8)),
            dma((2, 5, PIECES)),
            dma((2, 2, 3, 4, PIECES)),
        ],
        cost_estimate=pl.CostEstimate(flops=4 * total * rows * depth, bytes_accessed=4 * rows * depth, transcendentals=0),
        compiler_params=pltpu.CompilerParams(collective_id=0, has_side_effects=True, vmem_limit_bytes=60 << 20),
    )(hot1, hot0, emission, last, forward, transition)


def final_kernel(fall_ref, zall_ref, gw_ref, win_ref, u_ref, back_ref, count_ref):
    seqs = u_ref.shape[1]
    c = lax.axis_index("col")

    def work(h):
        parts = []
        for time in range(2):
            for src in range(8):
                value = fall_ref[time, src].astype(jnp.float32)[h * seqs:(h + 1) * seqs]
                parts.append(value * (1.0 / zall_ref[src, time, :, :1]))
        weight = jnp.concatenate(parts, axis=0).astype(jnp.bfloat16)
        totals = jnp.dot(gw_ref[...], weight, preferred_element_type=jnp.float32).T
        count_ref[...] = win_ref[...].astype(jnp.float32) * totals * (H * H / N)

    half = pl.program_id(1)
    for h in range(2):
        pl.when(half == h)(functools.partial(work, h))
    for time in range(2):
        back_ref[time] = u_ref[time] * (1.0 / zall_ref[c, time, :, :1])


def final_call(forward_all, zall, picked, transition, u):
    rows = transition.shape[0]
    seqs = u.shape[1]
    block = 2048
    tiles = rows // 2 // block
    return pl.pallas_call(
        final_kernel,
        grid=(tiles, 2),
        in_specs=[
            pl.BlockSpec((2, 8, 2 * seqs, block), lambda j, h: (0, 0, 0, j)),
            pl.BlockSpec(zall.shape, lambda j, h: (0, 0, 0, 0)),
            pl.BlockSpec(picked.shape, lambda j, h: (0, 0)),
            pl.BlockSpec((block, DW), lambda j, h: (h * tiles + j, 0)),
            pl.BlockSpec((2, seqs, block), lambda j, h: (0, 0, h * tiles + j)),
        ],
        out_specs=[
            pl.BlockSpec((2, seqs, block), lambda j, h: (0, 0, h * tiles + j)),
            pl.BlockSpec((block, DW), lambda j, h: (h * tiles + j, 0)),
        ],
        out_shape=[
            jax.ShapeDtypeStruct(u.shape, jnp.float32),
            jax.ShapeDtypeStruct((rows, DW), jnp.float32),
        ],
    )(forward_all, zall, picked, transition, u)


def fast_device(transition, emission, token_ids, forward, backward_last):
    row_index = lax.axis_index("row")
    row_seqs = backward_last.shape[0]
    seqs = forward.shape[1]
    tokens = lax.dynamic_slice_in_dim(token_ids[1], row_index * row_seqs, row_seqs, 0)
    hot1 = (tokens[:, None] == lax.broadcasted_iota(jnp.int32, (row_seqs, emission.shape[0]), 1)).astype(jnp.bfloat16)
    hot0 = (token_ids[0][:, None] == lax.broadcasted_iota(jnp.int32, (8 * seqs, emission.shape[0]), 1)).astype(jnp.bfloat16)
    u, zall, picked, forward_all = big_call(hot1, hot0, emission, backward_last, forward, transition)
    backward, counts = final_call(forward_all, zall, picked.reshape(16 * seqs, DW).T, transition, u)
    return (backward, counts)


def in_order(arrived, index):
    count = len(arrived)
    turned = jnp.stack([arrived[-i % count] for i in range(count)] * 2)
    return lax.dynamic_slice_in_dim(turned, (count - index) % count, count, 0)


def gather_small(value, col_count, col_index):
    arrived = [value]
    for k in range(1, col_count):
        arrived.append(lax.ppermute(value, "col", [(c, (c + k) % col_count) for c in range(col_count)]))
    place = lax.broadcasted_iota(jnp.int32, (col_count,) + value.shape, 0)
    out = jnp.zeros(place.shape, value.dtype)
    for k, got in enumerate(arrived):
        out = jnp.where(place == (col_index - k + col_count) % col_count, got[None], out)
    return out


def gather_rows(value, row_count, row_index):
    half = row_count // 2
    arrived = [value]
    for k in range(1, half):
        arrived.append(lax.ppermute(value, "row", [(r, (r + 2 * k) % row_count) for r in range(row_count)]))
    own = in_order(arrived, row_index // 2) if half > 1 else value[None]
    got = lax.ppermute(own, "row", [(r, r ^ 1) for r in range(row_count)])
    even = row_index % 2 == 0
    both = jnp.stack([jnp.where(even, own, got), jnp.where(even, got, own)], axis=1)
    return both.reshape(row_count * value.shape[0], value.shape[1])


def split_pair(partial, scale, col_count, col_index, local_seqs):
    scaled = (partial * scale).reshape(col_count // 2, 2, local_seqs, partial.shape[1])
    side = col_index % 2
    away = lax.dynamic_index_in_dim(scaled, 1 - side, 1, keepdims=False).astype(jnp.float16)
    return away, lax.dynamic_index_in_dim(scaled, side, 1, keepdims=False)


def reduce_scatter(away, keep, col_count, col_index):
    half = col_count // 2
    got = lax.ppermute(away, "col", [(c, c ^ 1) for c in range(col_count)])
    pair = keep + got.astype(jnp.float32)
    here = col_index // 2
    total = lax.dynamic_index_in_dim(pair, here, 0, keepdims=False)
    packed = pair.astype(jnp.float16)
    for k in range(1, half):
        piece = lax.dynamic_index_in_dim(packed, (here + k) % half, 0, keepdims=False)
        got = lax.ppermute(piece, "col", [(c, (c + 2 * k) % col_count) for c in range(col_count)])
        total = total + got.astype(jnp.float32)
    return total


def plain_product(weighted_back, transition, scale, scale_mine, col_count, col_index, local_seqs):
    chunk = transition.shape[0] // CHUNKS
    pieces = []
    for k in range(CHUNKS):
        rows = slice(k * chunk, (k + 1) * chunk)
        partial = lax.dot_general(
            weighted_back, transition[rows], (((1,), (1,)), ((), ())), preferred_element_type=jnp.float32
        )
        away, keep = split_pair(partial, scale, col_count, col_index, local_seqs)
        if k < CHUNKS - 1:
            weighted_back, away = lax.optimization_barrier((weighted_back, away))
        pieces.append(reduce_scatter(away, keep, col_count, col_index))
    return jnp.concatenate(pieces, axis=1) / scale_mine


def on_device(transition, emission, token_ids, forward, backward_last):
    row_count = lax.axis_size("row")
    col_count = lax.axis_size("col")
    row_index = lax.axis_index("row")
    col_index = lax.axis_index("col")
    ratio = col_count // row_count
    local_seqs = forward.shape[1]
    row_seqs = backward_last.shape[0]
    block_src = transition.shape[0]
    block_dst = transition.shape[1]
    seq_total = local_seqs * col_count
    columns = lax.broadcasted_iota(jnp.int32, (row_seqs, emission.shape[0]), 1)
    window = transition[:, :DW]
    outputs = [None, None]
    normals = [None, None]
    picked = [None, None]
    beta = backward_last
    scale = jnp.full((seq_total, 1), 64.0, jnp.float32)
    scale_mine = jnp.full((local_seqs, 1), 64.0, jnp.float32)
    for step in (1, 0):
        tokens = lax.dynamic_slice_in_dim(token_ids[step], row_index * row_seqs, row_seqs, 0)
        onehot = (tokens[:, None] == columns).astype(jnp.bfloat16)
        emitted = jnp.dot(onehot, emission, preferred_element_type=jnp.float32)
        local_back = (emitted * beta).astype(jnp.bfloat16)
        weighted_back = gather_rows(local_back, row_count, row_index)
        picked[step] = weighted_back[:, :DW]
        if step == 1:
            forward_all = lax.all_gather(forward, "col", axis=1, tiled=True)
        mine = plain_product(weighted_back, transition, scale, scale_mine, col_count, col_index, local_seqs)
        norm = jnp.sum(forward[step].astype(jnp.float32) * mine, axis=1)
        sums = lax.psum(jnp.stack([norm, jnp.sum(mine, axis=1)]), "row")
        sums_all = gather_small(sums, col_count, col_index)
        normals[step] = sums_all[:, 0].reshape(seq_total)
        outputs[step] = mine / sums[0][:, None]
        if step == 1:
            halves = outputs[step].reshape(local_seqs, ratio, block_dst)
            arrived = []
            for p in range(ratio):
                part = lax.dynamic_index_in_dim(halves, (col_index + p) % ratio, 1, keepdims=False)
                moves = []
                for r in range(row_count):
                    for c in range(col_count):
                        moves.append((r * col_count + c, (c // ratio) * col_count + r * ratio + (c + p) % ratio))
                arrived.append(lax.ppermute(part, ("row", "col"), moves))
            beta = in_order(arrived, col_index % ratio).reshape(row_seqs, block_dst)
            scale = (16777216.0 * sums_all[:, 0] / sums_all[:, 1]).reshape(seq_total, 1)
            scale_mine = (16777216.0 * sums[0] / sums[1])[:, None]
    totals = jnp.zeros((block_src, DW), jnp.float32)
    for step in (1, 0):
        scaled = (forward_all[step].astype(jnp.float32) / normals[step][:, None]).astype(jnp.bfloat16)
        totals = totals + lax.dot_general(
            scaled, picked[step], (((0,), (0,)), ((), ())), preferred_element_type=jnp.float32
        )
    counts = window.astype(jnp.float32) * totals * (H * H / N)
    return (jnp.stack(outputs), counts)


def solution(mesh):
    in_specs = (P("row", "col"), P(None, "col"), P(), P(None, "col", "row"), P("row", "col"))
    out_specs = (P(None, "col", "row"), P("row", "col"))
    fits = mesh.shape["row"] == 4 and mesh.shape["col"] == 8
    return jax.shard_map(
        fast_device if fits else on_device, mesh=mesh, in_specs=in_specs, out_specs=out_specs, check_vma=False
    )
```

```python
import functools
import math

import jax
import jax.numpy as jnp
from jax import lax
from jax.experimental import pallas as pl
from jax.experimental.pallas import tpu as pltpu
from jax.sharding import PartitionSpec as P

H = 32768
N = 192
DW = 128
CHUNKS = 2
A_MIN, A_MAX = 1.5258789e-06, 0.0024414062
E_MIN, E_MAX = 0.0099487305, 1.0
B_MIN, B_MAX = 0.1, 10.0
CHUNK = 512
SLOTS = 4
MESH = pl.DeviceIdType.MESH


def code_range(lo, hi):
    low = math.log2(lo) - 0.5
    high = math.log2(hi) + 0.5
    return 65000.0 / (high - low), (high + low) / 2


def encode(value, slope, middle):
    return jnp.round(jnp.log2(value) * slope - slope * middle).astype(jnp.int32).astype(jnp.int16)


def decode(code, slope, middle):
    return jnp.exp2(code.astype(jnp.int32).astype(jnp.float32) * (1.0 / slope) + middle)


def big_kernel(
    codes, hot1_ref, hot0_ref, emit_ref, last_ref, fwd_ref, a_ref,
    u_ref, zall_ref, gw_ref, fall_ref,
    a_buf, p_buf, q_buf, g1, g0, zacc, zs, zr, zc, us, ug,
    xs, xr, as_, ar, bs, br, cs, cr,
    a_sem, x_sem, al_sem, b_sem, c_sem, gy_sem, gc_sem, gd_sem, us_sem, ug_sem, uc_sem, zr_sem, zc_sem, fx_sem, fz_sem,
):
    count = xs.shape[1]
    slots, chunk = a_buf.shape[0], a_buf.shape[1]
    seqs = q_buf.shape[2]
    half = chunk // 2
    per = count // 2
    deep = q_buf.shape[0]
    r = lax.axis_index("row")
    c = lax.axis_index("col")
    y, k, z, x = r // 2, r % 2, c // 2, c % 2
    side = z // 2
    outer = (z == 0) | (z == 3)
    z_in, z_out = 1 + side, 3 * side
    z_in2, z_out2 = 2 - side, 3 - 3 * side
    px = 2 * z + 1 - x
    r1, r2 = r + 1 - 2 * k, (r + 2) % 4
    part_cols = g1.shape[2] // 4

    def remote(src, dst, send, recv, row, col):
        return pltpu.make_async_remote_copy(
            src_ref=src, dst_ref=dst, send_sem=send, recv_sem=recv,
            device_id={"row": row, "col": col}, device_id_type=MESH,
        )

    def load(g):
        slot = lax.rem(g, slots)
        n = lax.rem(g, count)
        at = pl.ds(pl.multiple_of(((n % 2) * per + n // 2) * chunk, chunk), chunk)
        return pltpu.make_async_copy(a_ref.at[at], a_buf.at[slot], a_sem.at[slot])

    for g in range(slots):
        load(g).start()
    barrier = pltpu.get_barrier_semaphore()
    me = r * 8 + c

    def greet(i, carry):
        @pl.when(i != me)
        def _():
            pl.semaphore_signal(barrier, inc=1, device_id={"row": i // 8, "col": i % 8}, device_id_type=MESH)
        return carry

    lax.fori_loop(0, 32, greet, 0)

    for j in range(4):
        cols = slice(j * part_cols, (j + 1) * part_cols)
        emitted = jnp.dot(hot1_ref[...], emit_ref[:, cols], preferred_element_type=jnp.float32)
        g1[r, :, cols] = (emitted * last_ref[:, cols]).astype(jnp.bfloat16)
    wide = fall_ref.shape[3]
    for time in range(2):
        for j in range(4):
            left = slice(j * wide // 4, (j + 1) * wide // 4)
            right = slice(wide + j * wide // 4, wide + (j + 1) * wide // 4)
            pair = [fwd_ref[time, :, left].astype(jnp.float32), fwd_ref[time, :, right].astype(jnp.float32)]
            fall_ref[time, c, :, left] = jnp.concatenate(pair, axis=0).astype(jnp.bfloat16)
    pl.semaphore_wait(barrier, 31)

    def g_move(block, j, sem, to):
        at = g1.at[block, :, pl.ds(j * part_cols, part_cols)]
        return remote(at, at, sem.at[0, j], sem.at[1, j], to, c)

    for j in range(4):
        g_move(r, j, gy_sem, r2).start()
        g_move(r, j, gc_sem, r1).start()

    bit = fall_ref.shape[3] // PIECES

    def piece(t, block, p):
        return fall_ref.at[t, block, :, pl.ds(pl.multiple_of(p * bit, bit), bit)]

    def fx_move(i, t, block, p):
        at = piece(t, block, p)
        return remote(at, at, fx_sem.at[0, i, p], fx_sem.at[1, i, p], r, px)

    def fz_move(way, kind, src, to, p):
        t = 0 if kind == 0 else 1
        at = piece(t, 2 * src + (x if kind < 2 else 1 - x), p)
        return remote(at, at, fz_sem.at[0, way, kind, src, p], fz_sem.at[1, way, kind, src, p], r, 2 * to + x)

    def fz_send(kind, d, p, act=lambda move: move.start()):
        @pl.when((z < 3) & (z - d + 1 >= 0))
        def _():
            act(fz_move(0, kind, z - d + 1, z + 1, p))

        @pl.when((z > 0) & (z + d - 1 <= 3))
        def _():
            act(fz_move(1, kind, z + d - 1, z - 1, p))

    def fz_got(kind, d, p):
        @pl.when(z - d >= 0)
        def _():
            fz_move(0, kind, z - d, z, p).wait_recv()

        @pl.when(z + d <= 3)
        def _():
            fz_move(1, kind, z + d, z, p).wait_recv()

    def fx_each(d, act, p):
        @pl.when(z - d >= 0)
        def _():
            act(fx_move(1 + z - d, 0, 2 * (z - d) + x, p))

        if d:
            @pl.when(z + d <= 3)
            def _():
                act(fx_move(1 + z + d, 0, 2 * (z + d) + x, p))

    def start(move):
        move.start()

    def onward(kinds, d, p):
        for kind in kinds:
            if d > 1:
                fz_got(kind, d - 1, p)
            if d < 4:
                fz_send(kind, d, p)

    def pair_lines(p):
        fx_move(0, 1, c, p).wait_recv()
        onward((1, 2), 1, p)

    acts = {
        "pair": lambda p: fx_move(0, 1, c, p).start(), "one1": lambda p: onward((0,), 1, p),
        "one2": lambda p: onward((0,), 2, p), "one3": lambda p: onward((0,), 3, p), "one4": lambda p: onward((0,), 4, p),
        "two1": pair_lines, "two2": lambda p: onward((1, 2), 2, p), "two3": lambda p: onward((1, 2), 3, p),
        "own": lambda p: fx_each(0, start, p), "near": lambda p: fx_each(1, start, p), "mid": lambda p: fx_each(2, start, p),
        "far": lambda p: fx_each(3, start, p),
    }

    def whole(name):
        def body(p, carry):
            acts[name](p)
            return carry

        lax.fori_loop(0, PIECES, body, 0)

    for name in PLAN:
        whole(name)
    for j in range(4):
        g_move(r, j, gy_sem, r2).wait_recv()
        g_move(r2, j, gd_sem, r1).start()
    for j in range(4):
        g_move(r, j, gc_sem, r1).wait()
        g_move(r2, j, gd_sem, r1).wait()
        g_move(r, j, gy_sem, r2).wait_send()

    def two(value):
        return jnp.concatenate([value[:, :half], value[:, half:]], axis=0)

    def one(value):
        n = value.shape[0] // 2
        return jnp.concatenate([value[:n], value[n:]], axis=1)

    zacc[...] = jnp.zeros(zacc.shape, jnp.float32)

    def run(ti, g_buf, ticks):
        time = 1 - ti
        slope, middle = codes[ti]
        enc = functools.partial(encode, slope=slope, middle=middle)
        dec = functools.partial(decode, slope=slope, middle=middle)

        def x_move(n):
            return remote(xs.at[ti, n], xr.at[ti, n], x_sem.at[0, ti, n], x_sem.at[1, ti, n], r, px)

        def a_move(n):
            return remote(as_.at[ti, n], ar.at[ti, n], al_sem.at[0, ti, n], al_sem.at[1, ti, n], r, 2 * z_in + x)

        def b_move(n):
            return remote(bs.at[ti, n], br.at[ti, n], b_sem.at[0, ti, n], b_sem.at[1, ti, n], r, 2 * z_in2 + x)

        def c_move(n):
            return remote(cs.at[ti, n], cr.at[ti, n], c_sem.at[0, ti, n], c_sem.at[1, ti, n], r, 2 * z_out + x)

        def u_move(n, yy, to_col, q):
            return remote(us.at[n], ug.at[q, c], us_sem.at[yy, n], ug_sem.at[q, c], 2 * yy + k, to_col)

        def uc_move(q):
            return remote(ug.at[q], ug.at[q], uc_sem.at[0, q], uc_sem.at[1, q], r1, c)

        def body(m, carry):
            @pl.when(m < count)
            def _():
                g = m + ti * count
                load(g).wait()
                part = lax.dot_general(
                    g_buf[...].reshape(8 * seqs, g_buf.shape[-1]), a_buf[lax.rem(g, slots)], (((1,), (1,)), ((), ())),
                    preferred_element_type=jnp.float32,
                )
                p_buf[...] = part.reshape(p_buf.shape)

                @pl.when(g + slots < 2 * count)
                def _():
                    load(g + slots).start()

                xs[ti, m] = enc(p_buf[:, 1 - x].reshape(4 * seqs, chunk))
                x_move(m).start()
                q_buf[lax.rem(m, deep)] = p_buf[:, x]

            for at, name in ticks:
                pl.when((m >= at) & (m < at + PIECES))(functools.partial(acts[name], m - at))

            @pl.when((m >= LAG) & (m < count + LAG))
            def _():
                n = m - LAG
                s = lax.rem(n, deep)
                x_move(n).wait()
                q_buf[s] += dec(xr[ti, n]).reshape(4, seqs, chunk)

                @pl.when(outer)
                def _():
                    three = jnp.concatenate([q_buf[s, z_in], q_buf[s, z_in2], q_buf[s, z_out2]], axis=0)
                    as_[ti, n] = enc(two(three))
                    a_move(n).start()

            @pl.when((m >= 2 * LAG) & (m < count + 2 * LAG) & jnp.logical_not(outer))
            def _():
                n = m - 2 * LAG
                s = lax.rem(n, deep)
                a_move(n).wait_recv()
                got = one(dec(ar[ti, n]))
                q_buf[s, z_in] += got[:seqs]
                pair = jnp.concatenate([q_buf[s, z_in2] + got[seqs:2 * seqs], q_buf[s, z_out2] + got[2 * seqs:]], axis=0)
                bs[ti, n] = enc(pair)
                b_move(n).start()

            @pl.when((m >= 3 * LAG) & (m < count + 3 * LAG) & jnp.logical_not(outer))
            def _():
                n = m - 3 * LAG
                s = lax.rem(n, deep)
                b_move(n).wait()
                got = dec(br[ti, n])
                q_buf[s, z_in] += got[:seqs]
                cs[ti, n] = enc(two(q_buf[s, z_out] + got[seqs:]))
                c_move(n).start()

            @pl.when((m >= 4 * LAG) & (m < count + 4 * LAG))
            def _():
                n = m - 4 * LAG
                s = lax.rem(n, deep)

                @pl.when(outer)
                def _():
                    c_move(n).wait_recv()
                    a_move(n).wait_send()
                    q_buf[s, z_out] += one(dec(cr[ti, n]))

                @pl.when(jnp.logical_not(outer))
                def _():
                    c_move(n).wait_send()

                value = q_buf[s, z]
                cols = pl.ds(pl.multiple_of(((n % 2) * per + n // 2) * chunk, chunk), chunk)
                u_ref[time, :, cols] = value
                weighed = fwd_ref[time, :, cols].astype(jnp.float32) * value
                total = zacc[time]
                for i in range(chunk // 128):
                    total = total + weighed[:, i * 128:(i + 1) * 128]
                zacc[time] = total
                if ti == 0:
                    h = n % 2
                    q = n // 2
                    to_col = 2 * r + h
                    us[n] = enc(two(value))
                    for yy in range(2):
                        mine = (yy == y) & (to_col == c)

                        @pl.when(mine)
                        def _():
                            ug[q, c] = us[n]

                        @pl.when(jnp.logical_not(mine))
                        def _():
                            u_move(n, yy, to_col, q).start()

            if ti == 0:
                ahead = m - (4 * LAG + GAP + x)
                direct = k == z % 2

                @pl.when((ahead >= 0) & (ahead < 2 * per) & (ahead % 2 == 0) & direct)
                def _():
                    q = ahead // 2
                    for src in range(8):
                        @pl.when(jnp.logical_not((r == z) & (c == src)))
                        def _():
                            remote(us.at[0], ug.at[q, src], us_sem.at[0, 0], ug_sem.at[q, src], r, src).wait_recv()
                    uc_move(q).start()

                later = ahead - GAP2

                @pl.when((later >= 0) & (later < 2 * per) & (later % 2 == 0))
                def _():
                    q = later // 2

                    @pl.when(direct)
                    def _():
                        uc_move(q).wait_send()

                    @pl.when(jnp.logical_not(direct))
                    def _():
                        uc_move(q).wait_recv()

                    cols = pl.ds(pl.multiple_of(q * chunk, chunk), chunk)
                    emitted = jnp.dot(hot0_ref[...], emit_ref[:, cols], preferred_element_type=jnp.float32)
                    for src in range(8):
                        value = one(dec(ug[q, src])) * emitted[src * seqs:(src + 1) * seqs]
                        p_buf[src // 2, src % 2] = value
                    g0[:, cols] = p_buf[...].reshape(8 * seqs, chunk).astype(jnp.bfloat16)

            return carry

        steps = count + 4 * LAG
        if ti == 0:
            steps += GAP + GAP2
        lax.fori_loop(0, steps, body, 0)
        if ti == 1:
            def sent(n, carry):
                h = n % 2
                for yy in range(2):
                    mine = (yy == y) & (2 * r + h == c)

                    @pl.when(jnp.logical_not(mine))
                    def _():
                        u_move(n, yy, 2 * r + h, n // 2).wait_send()
                return carry

            lax.fori_loop(0, count, sent, 0)

    def z_move(time, d):
        return remote(zs.at[time], zr.at[time, d], zr_sem.at[0, time, d], zr_sem.at[1, time, d], lax.rem(r + d, 4), c)

    def z_start(time):
        zs[time] = jnp.broadcast_to(jnp.sum(zacc[time], axis=1, keepdims=True), zs.shape[1:])
        for d in range(1, 4):
            z_move(time, d).start()

    run(0, g1, PLAN1)
    z_start(1)
    run(1, g0, PLAN0)
    z_start(0)
    gw_ref[1] = g1[:, :, :128].reshape(8 * seqs, 128)
    gw_ref[0] = g0[:, :128]
    def zc_move(time, d):
        return remote(zc.at[time], zall_ref.at[c, time], zc_sem.at[0, time, d], zc_sem.at[1, time, d], r, lax.rem(c + d, 8))

    def z_spread(time):
        for d in range(1, 4):
            z_move(time, d).wait()
        zr[time, 0] = zs[time]

        def arrived(i):
            return zr[time, lax.rem(r + 4 - i, 4)]

        zc[time] = (arrived(0) + arrived(1)) + (arrived(2) + arrived(3))
        zall_ref[c, time] = zc[time]
        for d in range(1, 8):
            zc_move(time, d).start()

    z_spread(1)
    z_spread(0)
    def finish(p, carry):
        for kind in (1, 2):
            fz_got(kind, 3, p)
        for kind in range(3):
            for d in (1, 2, 3):
                fz_send(kind, d, p, lambda move: move.wait_send())
        fx_move(0, 1, c, p).wait_send()
        for d in range(4):
            fx_each(d, lambda move: move.wait_send(), p)
        for src in range(4):
            fx_move(1 + src, 0, 2 * src + x, p).wait_recv()
        return carry

    lax.fori_loop(0, PIECES, finish, 0)
    for time in range(2):
        for d in range(1, 8):
            zc_move(time, d).wait()


LAG = 2
GAP = 3
GAP2 = 2


PIECES = 8
PLAN = ("pair", "one1")
PLAN1 = ((0, "one2"), (5, "one3"), (14, "own"))
PLAN0 = ((0, "one4"), (0, "two1"), (8, "two2"), (16, "near"), (16, "two3"), (16, "mid"), (16, "far"))


def big_call(hot1, hot0, emission, last, forward, transition):
    rows, depth = transition.shape
    seqs = forward.shape[1]
    chunk = CHUNK
    count = rows // chunk
    total = 8 * seqs
    i16, f32, bf16 = jnp.int16, jnp.float32, jnp.bfloat16
    lo1, hi1 = depth * A_MIN * E_MIN * B_MIN, H * A_MAX * E_MAX * B_MAX
    lo0, hi0 = depth * A_MIN * E_MIN * (H * A_MIN * E_MIN * B_MIN), H * A_MAX * E_MAX * hi1
    codes = (code_range(lo1, hi1), code_range(lo0, hi0))
    dma = pltpu.SemaphoreType.DMA
    vmem = pl.BlockSpec(memory_space=pltpu.VMEM)
    anyw = pl.BlockSpec(memory_space=pl.ANY)
    return pl.pallas_call(
        functools.partial(big_kernel, codes),
        out_shape=(
            jax.ShapeDtypeStruct((2, seqs, rows), f32),
            jax.ShapeDtypeStruct((8, 2, seqs, 128), f32),
            jax.ShapeDtypeStruct((2, total, 128), bf16),
            jax.ShapeDtypeStruct((2, 8, 2 * seqs, rows // 2), bf16),
        ),
        in_specs=[vmem] * 5 + [anyw],
        out_specs=(vmem, vmem, vmem, vmem),
        scratch_shapes=[
            pltpu.VMEM((SLOTS, chunk, depth), bf16),
            pltpu.VMEM((4, 2, seqs, chunk), f32),
            pltpu.VMEM((4 * LAG + 1, 4, seqs, chunk), f32),
            pltpu.VMEM((4, 2 * seqs, depth), bf16),
            pltpu.VMEM((total, depth), bf16),
            pltpu.VMEM((2, seqs, 128), f32),
            pltpu.VMEM((2, seqs, 128), f32),
            pltpu.VMEM((2, 4, seqs, 128), f32),
            pltpu.VMEM((2, seqs, 128), f32),
            pltpu.VMEM((count, 2 * seqs, chunk // 2), i16),
            pltpu.VMEM((count // 2, 8, 2 * seqs, chunk // 2), i16),
            pltpu.VMEM((2, count, 4 * seqs, chunk), i16),
            pltpu.VMEM((2, count, 4 * seqs, chunk), i16),
            pltpu.VMEM((2, count, 6 * seqs, chunk // 2), i16),
            pltpu.VMEM((2, count, 6 * seqs, chunk // 2), i16),
            pltpu.VMEM((2, count, 2 * seqs, chunk), i16),
            pltpu.VMEM((2, count, 2 * seqs, chunk), i16),
            pltpu.VMEM((2, count, 2 * seqs, chunk // 2), i16),
            pltpu.VMEM((2, count, 2 * seqs, chunk // 2), i16),
            dma((SLOTS,)),
            dma((2, 2, count)),
            dma((2, 2, count)),
            dma((2, 2, count)),
            dma((2, 2, count)),
            dma((2, 4)),
            dma((2, 4)),
            dma((2, 4)),
            dma((2, count)),
            dma((count // 2, 8)),
            dma((2, count // 2)),
            dma((2, 2, 4)),
            dma((2, 2, 8)),
            dma((2, 5, PIECES)),
            dma((2, 2, 3, 4, PIECES)),
        ],
        cost_estimate=pl.CostEstimate(flops=4 * total * rows * depth, bytes_accessed=4 * rows * depth, transcendentals=0),
        compiler_params=pltpu.CompilerParams(collective_id=0, has_side_effects=True, vmem_limit_bytes=60 << 20),
    )(hot1, hot0, emission, last, forward, transition)


def final_kernel(fall_ref, zall_ref, gw_ref, win_ref, u_ref, back_ref, count_ref):
    seqs = u_ref.shape[1]
    c = lax.axis_index("col")

    def work(h):
        parts = []
        for time in range(2):
            for src in range(8):
                value = fall_ref[time, src].astype(jnp.float32)[h * seqs:(h + 1) * seqs]
                parts.append(value * (1.0 / zall_ref[src, time, :, :1]))
        weight = jnp.concatenate(parts, axis=0).astype(jnp.bfloat16)
        totals = jnp.dot(gw_ref[...], weight, preferred_element_type=jnp.float32).T
        count_ref[...] = win_ref[...].astype(jnp.float32) * totals * (H * H / N)

    half = pl.program_id(1)
    for h in range(2):
        pl.when(half == h)(functools.partial(work, h))
    for time in range(2):
        back_ref[time] = u_ref[time] * (1.0 / zall_ref[c, time, :, :1])


def final_call(forward_all, zall, picked, transition, u):
    rows = transition.shape[0]
    seqs = u.shape[1]
    block = 2048
    tiles = rows // 2 // block
    return pl.pallas_call(
        final_kernel,
        grid=(tiles, 2),
        in_specs=[
            pl.BlockSpec((2, 8, 2 * seqs, block), lambda j, h: (0, 0, 0, j)),
            pl.BlockSpec(zall.shape, lambda j, h: (0, 0, 0, 0)),
            pl.BlockSpec(picked.shape, lambda j, h: (0, 0)),
            pl.BlockSpec((block, DW), lambda j, h: (h * tiles + j, 0)),
            pl.BlockSpec((2, seqs, block), lambda j, h: (0, 0, h * tiles + j)),
        ],
        out_specs=[
            pl.BlockSpec((2, seqs, block), lambda j, h: (0, 0, h * tiles + j)),
            pl.BlockSpec((block, DW), lambda j, h: (h * tiles + j, 0)),
        ],
        out_shape=[
            jax.ShapeDtypeStruct(u.shape, jnp.float32),
            jax.ShapeDtypeStruct((rows, DW), jnp.float32),
        ],
    )(forward_all, zall, picked, transition, u)


def fast_device(transition, emission, token_ids, forward, backward_last):
    row_index = lax.axis_index("row")
    row_seqs = backward_last.shape[0]
    seqs = forward.shape[1]
    tokens = lax.dynamic_slice_in_dim(token_ids[1], row_index * row_seqs, row_seqs, 0)
    hot1 = (tokens[:, None] == lax.broadcasted_iota(jnp.int32, (row_seqs, emission.shape[0]), 1)).astype(jnp.bfloat16)
    hot0 = (token_ids[0][:, None] == lax.broadcasted_iota(jnp.int32, (8 * seqs, emission.shape[0]), 1)).astype(jnp.bfloat16)
    u, zall, picked, forward_all = big_call(hot1, hot0, emission, backward_last, forward, transition)
    backward, counts = final_call(forward_all, zall, picked.reshape(16 * seqs, DW).T, transition, u)
    return (backward, counts)


def in_order(arrived, index):
    count = len(arrived)
    turned = jnp.stack([arrived[-i % count] for i in range(count)] * 2)
    return lax.dynamic_slice_in_dim(turned, (count - index) % count, count, 0)


def gather_small(value, col_count, col_index):
    arrived = [value]
    for k in range(1, col_count):
        arrived.append(lax.ppermute(value, "col", [(c, (c + k) % col_count) for c in range(col_count)]))
    place = lax.broadcasted_iota(jnp.int32, (col_count,) + value.shape, 0)
    out = jnp.zeros(place.shape, value.dtype)
    for k, got in enumerate(arrived):
        out = jnp.where(place == (col_index - k + col_count) % col_count, got[None], out)
    return out


def gather_rows(value, row_count, row_index):
    half = row_count // 2
    arrived = [value]
    for k in range(1, half):
        arrived.append(lax.ppermute(value, "row", [(r, (r + 2 * k) % row_count) for r in range(row_count)]))
    own = in_order(arrived, row_index // 2) if half > 1 else value[None]
    got = lax.ppermute(own, "row", [(r, r ^ 1) for r in range(row_count)])
    even = row_index % 2 == 0
    both = jnp.stack([jnp.where(even, own, got), jnp.where(even, got, own)], axis=1)
    return both.reshape(row_count * value.shape[0], value.shape[1])


def split_pair(partial, scale, col_count, col_index, local_seqs):
    scaled = (partial * scale).reshape(col_count // 2, 2, local_seqs, partial.shape[1])
    side = col_index % 2
    away = lax.dynamic_index_in_dim(scaled, 1 - side, 1, keepdims=False).astype(jnp.float16)
    return away, lax.dynamic_index_in_dim(scaled, side, 1, keepdims=False)


def reduce_scatter(away, keep, col_count, col_index):
    half = col_count // 2
    got = lax.ppermute(away, "col", [(c, c ^ 1) for c in range(col_count)])
    pair = keep + got.astype(jnp.float32)
    here = col_index // 2
    total = lax.dynamic_index_in_dim(pair, here, 0, keepdims=False)
    packed = pair.astype(jnp.float16)
    for k in range(1, half):
        piece = lax.dynamic_index_in_dim(packed, (here + k) % half, 0, keepdims=False)
        got = lax.ppermute(piece, "col", [(c, (c + 2 * k) % col_count) for c in range(col_count)])
        total = total + got.astype(jnp.float32)
    return total


def plain_product(weighted_back, transition, scale, scale_mine, col_count, col_index, local_seqs):
    chunk = transition.shape[0] // CHUNKS
    pieces = []
    for k in range(CHUNKS):
        rows = slice(k * chunk, (k + 1) * chunk)
        partial = lax.dot_general(
            weighted_back, transition[rows], (((1,), (1,)), ((), ())), preferred_element_type=jnp.float32
        )
        away, keep = split_pair(partial, scale, col_count, col_index, local_seqs)
        if k < CHUNKS - 1:
            weighted_back, away = lax.optimization_barrier((weighted_back, away))
        pieces.append(reduce_scatter(away, keep, col_count, col_index))
    return jnp.concatenate(pieces, axis=1) / scale_mine


def on_device(transition, emission, token_ids, forward, backward_last):
    row_count = lax.axis_size("row")
    col_count = lax.axis_size("col")
    row_index = lax.axis_index("row")
    col_index = lax.axis_index("col")
    ratio = col_count // row_count
    local_seqs = forward.shape[1]
    row_seqs = backward_last.shape[0]
    block_src = transition.shape[0]
    block_dst = transition.shape[1]
    seq_total = local_seqs * col_count
    columns = lax.broadcasted_iota(jnp.int32, (row_seqs, emission.shape[0]), 1)
    window = transition[:, :DW]
    outputs = [None, None]
    normals = [None, None]
    picked = [None, None]
    beta = backward_last
    scale = jnp.full((seq_total, 1), 64.0, jnp.float32)
    scale_mine = jnp.full((local_seqs, 1), 64.0, jnp.float32)
    for step in (1, 0):
        tokens = lax.dynamic_slice_in_dim(token_ids[step], row_index * row_seqs, row_seqs, 0)
        onehot = (tokens[:, None] == columns).astype(jnp.bfloat16)
        emitted = jnp.dot(onehot, emission, preferred_element_type=jnp.float32)
        local_back = (emitted * beta).astype(jnp.bfloat16)
        weighted_back = gather_rows(local_back, row_count, row_index)
        picked[step] = weighted_back[:, :DW]
        if step == 1:
            forward_all = lax.all_gather(forward, "col", axis=1, tiled=True)
        mine = plain_product(weighted_back, transition, scale, scale_mine, col_count, col_index, local_seqs)
        norm = jnp.sum(forward[step].astype(jnp.float32) * mine, axis=1)
        sums = lax.psum(jnp.stack([norm, jnp.sum(mine, axis=1)]), "row")
        sums_all = gather_small(sums, col_count, col_index)
        normals[step] = sums_all[:, 0].reshape(seq_total)
        outputs[step] = mine / sums[0][:, None]
        if step == 1:
            halves = outputs[step].reshape(local_seqs, ratio, block_dst)
            arrived = []
            for p in range(ratio):
                part = lax.dynamic_index_in_dim(halves, (col_index + p) % ratio, 1, keepdims=False)
                moves = []
                for r in range(row_count):
                    for c in range(col_count):
                        moves.append((r * col_count + c, (c // ratio) * col_count + r * ratio + (c + p) % ratio))
                arrived.append(lax.ppermute(part, ("row", "col"), moves))
            beta = in_order(arrived, col_index % ratio).reshape(row_seqs, block_dst)
            scale = (16777216.0 * sums_all[:, 0] / sums_all[:, 1]).reshape(seq_total, 1)
            scale_mine = (16777216.0 * sums[0] / sums[1])[:, None]
    totals = jnp.zeros((block_src, DW), jnp.float32)
    for step in (1, 0):
        scaled = (forward_all[step].astype(jnp.float32) / normals[step][:, None]).astype(jnp.bfloat16)
        totals = totals + lax.dot_general(
            scaled, picked[step], (((0,), (0,)), ((), ())), preferred_element_type=jnp.float32
        )
    counts = window.astype(jnp.float32) * totals * (H * H / N)
    return (jnp.stack(outputs), counts)


def solution(mesh):
    in_specs = (P("row", "col"), P(None, "col"), P(), P(None, "col", "row"), P("row", "col"))
    out_specs = (P(None, "col", "row"), P("row", "col"))
    fits = mesh.shape["row"] == 4 and mesh.shape["col"] == 8
    return jax.shard_map(
        fast_device if fits else on_device, mesh=mesh, in_specs=in_specs, out_specs=out_specs, check_vma=False
    )
```
